256 devices in a mesh: pb: 32 (over z, y_hi, core), ka: 8 (over x, y_lo).
Axes of the slice: x: 4, y: 4 (y_hi: 2, y_lo: 2; y = y_hi * 2 + y_lo), z: 8, core: 2. Of those that a mesh axis runs over, the one named last changes fastest.
Arguments:
- queries: bfloat16 [32768, 128], P(('pb', 'ka')), may hold values from -4 to 4
- key_rows: bfloat16 [32768, 128], P(('pb', 'ka')), may hold values from -4 to 4
- value_rows: bfloat16 [32768, 128], P(('pb', 'ka')), may hold values from -6 to 6
- outputs: bfloat16 [32768, 128], P(('pb', 'ka')), may hold values from -3 to 3
- out_grad: bfloat16 [32768, 128], P(('pb', 'ka')), may hold values from -6 to 6
- log_sums: float32 [32768], P(('pb', 'ka')), may hold values from 3 to 6
- doc_lengths: int32 [16], replicated, may hold values from 1 to 24576, 32768 in all
- tile_allowed: int32 [16, 16], replicated, may hold values from 0 to 1, as said below
Outputs:
- query_grad: bfloat16 [32768, 128], P(('pb', 'ka'))
- key_grad: bfloat16 [32768, 128], P(('pb', 'ka'))
- value_grad: bfloat16 [32768, 128], P(('pb', 'ka'))
The draws below stay inside these ranges and needn't reach their ends.
Inputs may be any that keep to these rules, and one draw needn't show every extreme that they name: tile_allowed is 1 on the diagonal and 0 above it.
All inputs are finite; a program needn't handle non-finite values.
Results may differ from the reference program's by a relative error of at most 0.02.
Values may be sent and summed in bfloat16 or wider, within the bound.
No kernel may reach another device: no remote copies, remote signals or barrier semaphores. Data moves between devices by JAX's collectives and lax.ppermute only.
A program may use at most 64 MiB of HBM per device.

```python
import math
import jax
import jax.numpy as jnp
import numpy as np
from jax import lax

HEAD = 128
TILE = 2048
NDOCS = 16
SEQ = 32768
NTILES = 16
DOCMOST = 24576


def draw_tile_allowed(key, part):
    key = jax.random.fold_in(key, 7)
    random_bits = jax.random.randint(key, (NTILES, NTILES), 0, 2, dtype=jnp.int32)
    row_ids = jnp.arange(NTILES, dtype=jnp.int32)[:, None]
    col_ids = jnp.arange(NTILES, dtype=jnp.int32)[None, :]
    return jnp.where(col_ids == row_ids, 1, jnp.where(col_ids < row_ids, random_bits, 0)).astype(jnp.int32)


def block_levels(rng, dims, shards, least, top_value):
    level = 1.0
    for dim, shards_of in shards:
        draws = jax.random.uniform(jax.random.fold_in(jax.random.fold_in(rng, 6), dim), (shards_of,), jnp.float32, least / len(shards), top_value / len(shards))
        level = level * jnp.repeat(jnp.exp(draws), dims[dim] // shards_of).reshape((-1,) + (1,) * (len(dims) - 1 - dim))
    return level


def length_profile(number_of, total, limit, skew):
    portions = [(1 << 20) // math.isqrt(rank ** skew) + 1 for rank in range(2, number_of + 1)]
    spare, holding = total - limit - (number_of - 1), [1] * (number_of - 1)
    while spare > 0:
        movable = [i for i in range(number_of - 1) if holding[i] < limit]
        whole, budget = sum([portions[i] for i in movable]), spare
        for i in movable:
            addition = min(limit - holding[i], max(1, budget * portions[i] // whole), spare)
            holding[i] = holding[i] + addition
            spare = spare - addition
    return np.array([limit] + holding)


def uneven_parts(rng, number_of, total, reach, slope):
    if number_of == 2:
        one = jax.random.randint(rng, (), max(1, total - reach), min(reach, total - 1) + 1)
        return jnp.stack([one, total - one])
    sizes = jnp.asarray(length_profile(number_of, total, reach, slope), jnp.int32)
    pairs = (number_of - 1) // 2
    giver, sink = sizes[1:1 + 2 * pairs:2], sizes[2:2 + 2 * pairs:2]
    room = jnp.minimum(giver - 1, reach - sink)
    moved = jax.random.randint(jax.random.fold_in(rng, 1), (pairs,), 0, 1 << 20) % (room + 1)
    sizes = sizes.at[1:1 + 2 * pairs:2].set(giver - moved).at[2:2 + 2 * pairs:2].set(sink + moved)
    return sizes[jax.random.permutation(jax.random.fold_in(rng, 2), number_of)]


def gaussian(own_key, shape, width, bound, cuts=(), kind=jnp.bfloat16):
    factor_of = block_levels(own_key, shape, cuts, -0.22, 0.18) if cuts else 1.0
    result = jax.random.normal(own_key, shape, jnp.float32) * width * factor_of
    return jnp.minimum(jnp.maximum(result, -bound), bound).astype(kind)


def setup_inputs(seed: int = 0) -> dict:
    arg_keys = jax.random.split(jax.random.key(seed), 9)
    return {
        "queries": gaussian(arg_keys[0], (SEQ, HEAD), 1.0, 4.0, ((0, 256),)),
        "key_rows": gaussian(arg_keys[1], (SEQ, HEAD), 1.0, 4.0, ((0, 256),)),
        "value_rows": gaussian(arg_keys[2], (SEQ, HEAD), 1.0, 6.0, ((0, 256),)),
        "outputs": gaussian(arg_keys[3], (SEQ, HEAD), 0.5, 3.0, ((0, 256),)),
        "out_grad": gaussian(arg_keys[4], (SEQ, HEAD), 1.0, 6.0, ((0, 256),)),
        "log_sums": jnp.clip(3.0 + 3.0 * jax.random.uniform(arg_keys[5], (SEQ,), jnp.float32) ** block_levels(arg_keys[5], (SEQ,), ((0, 256),), -0.2, 0.2), 3.0, 6.0),
        "doc_lengths": uneven_parts(arg_keys[6], NDOCS, SEQ, DOCMOST, 2).astype(jnp.int32),
        "tile_allowed": draw_tile_allowed(jax.random.fold_in(arg_keys[8], 71), 0),
    }


def document_of(positions, doc_ends):
    return jnp.sum((positions[:, None] >= doc_ends[None, :]).astype(jnp.int32), axis=1)


def reference(queries, key_rows, value_rows, outputs, out_grad, log_sums, doc_lengths, tile_allowed):
    score_scale = HEAD ** -0.5
    doc_ends = jnp.cumsum(doc_lengths).astype(jnp.int32)
    row_delta = jnp.sum(out_grad.astype(jnp.float32) * outputs.astype(jnp.float32), axis=1)
    key_pos = jnp.arange(SEQ, dtype=jnp.int32)
    key_docs = document_of(key_pos, doc_ends)
    tile_ids = jnp.arange(NTILES, dtype=jnp.int32)
    key_tiles = (key_pos[:, None] // TILE == tile_ids[None, :]).astype(jnp.float32)
    allowed = tile_allowed.astype(jnp.float32)
    block_rows = min(SEQ, 1024)
    block_count = SEQ // block_rows

    def query_step(carry, index):
        key_acc, value_acc = carry
        start = (index * block_rows).astype(jnp.int32)
        q_part = lax.dynamic_slice_in_dim(queries, start, block_rows, 0)
        g_part = lax.dynamic_slice_in_dim(out_grad, start, block_rows, 0)
        lse_part = lax.dynamic_slice_in_dim(log_sums, start, block_rows, 0)
        delta_part = lax.dynamic_slice_in_dim(row_delta, start, block_rows, 0)
        positions = start + jnp.arange(block_rows, dtype=jnp.int32)
        doc_ids = document_of(positions, doc_ends)
        row_tiles = (positions[:, None] // TILE == tile_ids[None, :]).astype(jnp.float32)
        rows_ok = jnp.dot(row_tiles, allowed, precision=lax.Precision.HIGHEST)
        tile_ok = jnp.dot(rows_ok, key_tiles.T, precision=lax.Precision.HIGHEST) > 0.5
        visible = (positions[:, None] >= key_pos[None, :]) & (doc_ids[:, None] == key_docs[None, :]) & tile_ok
        scores = jnp.dot(q_part, key_rows.T, preferred_element_type=jnp.float32) * score_scale
        probs = jnp.where(visible, jnp.exp(scores - lse_part[:, None]), jnp.float32(0.0))
        probs_low = probs.astype(jnp.bfloat16)
        value_acc = value_acc + jnp.dot(probs_low.T, g_part, preferred_element_type=jnp.float32)
        prob_grad = jnp.dot(g_part, value_rows.T, preferred_element_type=jnp.float32)
        score_grad = (probs * (prob_grad - delta_part[:, None])).astype(jnp.bfloat16)
        query_part = jnp.dot(score_grad, key_rows, preferred_element_type=jnp.float32) * score_scale
        key_acc = key_acc + jnp.dot(score_grad.T, q_part, preferred_element_type=jnp.float32)
        return (key_acc, value_acc), query_part.astype(jnp.bfloat16)

    start_carry = (jnp.zeros((SEQ, HEAD), jnp.float32), jnp.zeros((SEQ, HEAD), jnp.float32))
    (key_acc, value_acc), query_parts = lax.scan(query_step, start_carry, jnp.arange(block_count, dtype=jnp.int32))
    query_grad = query_parts.reshape(SEQ, HEAD)
    key_grad = (key_acc * score_scale).astype(jnp.bfloat16)
    value_grad = value_acc.astype(jnp.bfloat16)
    return query_grad, key_grad, value_grad
```

```python
import functools
import math

import jax
import jax.numpy as jnp
from jax import lax
from jax.experimental import pallas as pl
from jax.experimental.pallas import tpu as pltpu
from jax.sharding import Mesh, PartitionSpec as P

AXES = ("z", "yh", "c", "x", "yl")
SIZES = (8, 2, 2, 4, 2)
ROWS = 128
WIDTH = 128
NDOCS = 16
TILE = 2048
RUN = 1024
CHUNK = 256
PACK = 272
LOG2E = math.log2(math.e)
SCALE = 128.0 ** -0.5


def split3(x):
    a = x.astype(jnp.bfloat16)
    r = x - a.astype(jnp.float32)
    b = r.astype(jnp.bfloat16)
    c = (r - b.astype(jnp.float32)).astype(jnp.bfloat16)
    return a, b, c


def pack_kernel(q_ref, g_ref, o_ref, lse_ref, out_ref):
    prod = g_ref[...].astype(jnp.float32) * o_ref[...].astype(jnp.float32)
    delta = jnp.sum(prod.T, axis=0, keepdims=True)
    lse2 = lse_ref[...] * LOG2E
    out_ref[0:128] = q_ref[...]
    out_ref[128:256] = g_ref[...]
    parts = split3(lse2) + split3(delta)
    stats = jnp.concatenate(
        [p.astype(jnp.float32) for p in parts] + [jnp.zeros((10, ROWS), jnp.float32)], axis=0
    )
    out_ref[256:272] = stats.astype(jnp.bfloat16)


def pack(q, g, o, lse):
    return pl.pallas_call(
        pack_kernel,
        out_shape=jax.ShapeDtypeStruct((PACK, WIDTH), jnp.bfloat16),
    )(q, g, o, lse)


def grad_kernel(
    where_ref, len_ref, allow_ref, own_ref, other_ref, kv_ref,
    dqo_ref, dqx_ref, dkv_ref, kt_ref, dk_acc, dv_acc, dqt_acc,
):
    z, yh, c, qoff = where_ref[0], where_ref[1], where_ref[2], where_ref[3]
    ends = []
    total = jnp.int32(0)
    for d in range(NDOCS):
        total = total + len_ref[d]
        ends.append(total)
    for r in range(2):
        k_run = kv_ref[8 * r : 8 * r + 8, 0:128, :].reshape(RUN, WIDTH)
        kt_ref[r] = k_run.T
    dk_acc[...] = jnp.zeros_like(dk_acc)
    dv_acc[...] = jnp.zeros_like(dv_acc)
    dqt_acc[...] = jnp.zeros_like(dqt_acc)

    def first_start(pos):
        s = jnp.int32(0)
        for e in ends:
            s = jnp.where(e <= pos, e, s)
        return s

    lane = lax.broadcasted_iota(jnp.int32, (1, 2 * ROWS), 1)

    def q_step(zq, carry):
        base = zq * (2 * TILE) + yh * TILE + qoff
        p_own = base + c * RUN
        p_other = base + (1 - c) * RUN
        s_own = first_start(p_own)
        s_other = first_start(p_other)
        pos = jnp.where(lane < ROWS, p_own + lane, p_other - ROWS + lane)
        start = jnp.zeros_like(pos)
        for e in ends:
            start = jnp.where(pos >= e, e, start)

        for r in range(2):
            b = z * (2 * TILE) + r * TILE + c * RUN
            ok = allow_ref[2 * zq + yh, 2 * z + r] == 1
            live_own = (s_own <= b + RUN - 1) & (b <= p_own + ROWS - 1)
            live_other = (s_other <= b + RUN - 1) & (b <= p_other + ROWS - 1)

            @pl.when(ok & (live_own | live_other))
            def _unit():
                q = jnp.concatenate([own_ref[zq, 0:128], other_ref[zq, 0:128]], axis=0)
                g = jnp.concatenate([own_ref[zq, 128:256], other_ref[zq, 128:256]], axis=0)
                st = jnp.concatenate(
                    [own_ref[zq, 256:272], other_ref[zq, 256:272]], axis=1
                ).astype(jnp.float32)
                lse2 = st[0:1] + st[1:2] + st[2:3]
                delta = st[3:4] + st[4:5] + st[5:6]
                dqt = dqt_acc[zq]
                for n in range(RUN // CHUNK):
                    blk = 8 * r + 2 * n
                    k = kv_ref[blk : blk + 2, 0:128, :].reshape(CHUNK, WIDTH)
                    v = kv_ref[blk : blk + 2, 128:256, :].reshape(CHUNK, WIDTH)
                    st_ = lax.dot_general(
                        k, q, (((1,), (1,)), ((), ())), preferred_element_type=jnp.float32
                    )
                    dp = lax.dot_general(
                        v, g, (((1,), (1,)), ((), ())), preferred_element_type=jnp.float32
                    )
                    key = (b + n * CHUNK) + lax.broadcasted_iota(
                        jnp.int32, (CHUNK, 2 * ROWS), 0
                    )
                    vis = (key >= start) & (key <= pos)
                    p = jnp.where(vis, jnp.exp2(st_ * (SCALE * LOG2E) - lse2), 0.0)
                    pb = p.astype(jnp.bfloat16)
                    ds = (p * (dp - delta)).astype(jnp.bfloat16)
                    rows = pl.ds(r * RUN + n * CHUNK, CHUNK)
                    dv_acc[rows] += jnp.dot(pb, g, preferred_element_type=jnp.float32)
                    dk_acc[rows] += jnp.dot(ds, q, preferred_element_type=jnp.float32)
                    dqt = dqt + jnp.dot(
                        kt_ref[r, :, n * CHUNK : (n + 1) * CHUNK],
                        ds,
                        preferred_element_type=jnp.float32,
                    )
                dqt_acc[zq] = dqt

        return carry

    lax.fori_loop(z, 8, q_step, 0)
    for zq in range(8):
        dq = dqt_acc[zq].T.astype(jnp.bfloat16)
        dqo_ref[zq] = dq[0:128]
        dqx_ref[zq] = dq[128:256]
    for blk in range(16):
        dkv_ref[blk, 0:128] = dk_acc[blk * ROWS : (blk + 1) * ROWS].astype(jnp.bfloat16)
        dkv_ref[blk, 128:256] = dv_acc[blk * ROWS : (blk + 1) * ROWS].astype(jnp.bfloat16)


def grads(where, doc_lengths, tile_allowed, own, other, kv):
    smem = pl.BlockSpec(memory_space=pltpu.SMEM)
    vmem = pl.BlockSpec(memory_space=pltpu.VMEM)
    bf = jnp.bfloat16
    return pl.pallas_call(
        grad_kernel,
        out_shape=(
            jax.ShapeDtypeStruct((8, ROWS, WIDTH), bf),
            jax.ShapeDtypeStruct((8, ROWS, WIDTH), bf),
            jax.ShapeDtypeStruct((16, 2 * ROWS, WIDTH), bf),
        ),
        in_specs=[smem, smem, smem, vmem, vmem, vmem],
        out_specs=(vmem, vmem, vmem),
        scratch_shapes=[
            pltpu.VMEM((2, WIDTH, RUN), bf),
            pltpu.VMEM((2 * RUN, WIDTH), jnp.float32),
            pltpu.VMEM((2 * RUN, WIDTH), jnp.float32),
            pltpu.VMEM((8, WIDTH, 2 * ROWS), jnp.float32),
        ],
        compiler_params=pltpu.CompilerParams(vmem_limit_bytes=32 * 1024 * 1024),
    )(where, doc_lengths, tile_allowed, own, other, kv)


def on_device(
    queries, key_rows, value_rows, outputs, out_grad, log_sums, doc_lengths, tile_allowed
):
    z, yh, c = lax.axis_index("z"), lax.axis_index("yh"), lax.axis_index("c")
    qoff = (lax.axis_index("x") * 2 + lax.axis_index("yl")) * ROWS
    where = jnp.stack([z, yh, c, qoff]).astype(jnp.int32)
    plane = ("yh", "x", "yl")
    swap = [(0, 1), (1, 0)]

    kv = jnp.concatenate([key_rows, value_rows], axis=0)
    kv_all = lax.all_to_all(
        jnp.broadcast_to(kv[None], (16, 2 * ROWS, WIDTH)), plane, 0, 0, tiled=True
    )
    qg = pack(queries, out_grad, outputs, log_sums.reshape(1, ROWS))
    own = lax.all_to_all(jnp.broadcast_to(qg[None], (8, PACK, WIDTH)), "z", 0, 0, tiled=True)
    other = lax.ppermute(own, "c", swap)
    dq_own, dq_other, dkv = grads(where, doc_lengths, tile_allowed, own, other, kv_all)
    dq_in = lax.ppermute(dq_other, "c", swap)
    dkv_in = lax.all_to_all(dkv, plane, 0, 0, tiled=True)
    dq_pair = (dq_own.astype(jnp.float32) + dq_in.astype(jnp.float32)).astype(jnp.bfloat16)
    dq_all = lax.all_to_all(dq_pair, "z", 0, 0, tiled=True)
    query_grad = (jnp.sum(dq_all.astype(jnp.float32), axis=0) * SCALE).astype(jnp.bfloat16)
    dkv_sum = jnp.sum(dkv_in.astype(jnp.float32), axis=0)
    key_grad = (dkv_sum[:ROWS] * SCALE).astype(jnp.bfloat16)
    value_grad = dkv_sum[ROWS:].astype(jnp.bfloat16)
    return query_grad, key_grad, value_grad


def solution(mesh):
    fine = Mesh(mesh.devices.reshape(SIZES), AXES)
    rows, vec = P(AXES, None), P(AXES)
    return jax.shard_map(
        on_device,
        mesh=fine,
        in_specs=(rows, rows, rows, rows, rows, vec, P(), P()),
        out_specs=(rows, rows, rows),
        check_vma=False,
    )
```

```python
import math

import jax
import jax.numpy as jnp
import numpy as np
from jax import lax
from jax.experimental import pallas as pl
from jax.experimental.pallas import tpu as pltpu
from jax.sharding import Mesh, PartitionSpec as P

AXES = ("z", "yh", "c", "x", "yl")
SIZES = (8, 2, 2, 4, 2)
PLANE = ("yh", "x", "yl")
ROWS = 128
WIDTH = 128
NDOCS = 16
TILE = 2048
RUN = 1024
CHUNK = 256
PACK = 272
FAR = 1 << 30
LOG2E = math.log2(math.e)
SCALE = 128.0 ** -0.5


def pairs_along_z(k, both_ways, back):
    pairs = []
    for i in range(256):
        z, yh, c, x, yl = (int(v) for v in np.unravel_index(i, SIZES))
        t = z - k + 8 if both_ways and c == 1 else z + k
        if z < t < 8:
            j = int(np.ravel_multi_index((t, yh, c, x, yl), SIZES))
            pairs.append((j, i) if back else (i, j))
    return pairs


def split3(x):
    a = x.astype(jnp.bfloat16)
    r = x - a.astype(jnp.float32)
    b = r.astype(jnp.bfloat16)
    c = (r - b.astype(jnp.float32)).astype(jnp.bfloat16)
    return a, b, c


def pack_kernel(q_ref, g_ref, o_ref, lse_ref, out_ref):
    prod = g_ref[...].astype(jnp.float32) * o_ref[...].astype(jnp.float32)
    delta = jnp.sum(prod.T, axis=0, keepdims=True)
    lse2 = lse_ref[...] * LOG2E
    parts = split3(lse2) + split3(delta)
    stats = jnp.concatenate(
        [p.astype(jnp.float32) for p in parts] + [jnp.zeros((10, ROWS), jnp.float32)], axis=0
    ).astype(jnp.bfloat16)
    for n in range(16):
        out_ref[n, 0:128] = q_ref[...]
        out_ref[n, 128:256] = g_ref[...]
        out_ref[n, 256:272] = stats


def pack(q, g, o, lse):
    return pl.pallas_call(
        pack_kernel,
        out_shape=jax.ShapeDtypeStruct((16, PACK, WIDTH), jnp.bfloat16),
    )(q, g, o, lse)


def grad_kernel(
    where_ref, len_ref, allow_ref, own_ref, other_ref, kv0_ref, kv4_ref, kv1_ref, kv2_ref, kv3_ref,
    dqo_ref, dqx_ref, d0_ref, d4_ref, d1_ref, d2_ref, d3_ref,
    k_s, v_s, kt_s, dk_acc, dv_acc, dqt_acc, stat_s, start_s, base_s,
):
    z, yh, c, koff = where_ref[0], where_ref[1], where_ref[2], where_ref[3]
    ends = []
    total = jnp.int32(0)
    for d in range(NDOCS):
        total = total + len_ref[d]
        ends.append(total)

    wide = ((kv1_ref, 1), (kv2_ref, 2), (kv3_ref, 3))
    for half, ref in enumerate((kv0_ref, kv4_ref)):
        k_s[0, half * ROWS : (half + 1) * ROWS] = ref[0:128]
        v_s[0, half * ROWS : (half + 1) * ROWS] = ref[128:256]
    for ref, s in wide:
        for half in range(2):
            k_s[s, half * ROWS : (half + 1) * ROWS] = ref[half, 0:128]
            v_s[s, half * ROWS : (half + 1) * ROWS] = ref[half, 128:256]
    for s in range(4):
        kt_s[s] = k_s[s].T
    dk_acc[...] = jnp.zeros_like(dk_acc)
    dv_acc[...] = jnp.zeros_like(dv_acc)
    dqt_acc[...] = jnp.zeros_like(dqt_acc)

    in_plane = yh * TILE + koff
    base_s[0] = z
    base_s[1] = z - 4
    for s in range(1, 4):
        zk = jnp.where(c == 0, z - s, z + s - 8)
        base_s[2 * s] = zk
        base_s[2 * s + 1] = zk

    lane = lax.broadcasted_iota(jnp.int32, (1, RUN), 1)
    for h, ref in enumerate((own_ref, other_ref)):
        cq = c if h == 0 else 1 - c
        for t in range(2):
            st = jnp.concatenate(
                [ref[8 * t + n, 256:272].astype(jnp.float32) for n in range(8)], axis=1
            )
            stat_s[2 * h + t, 0:1] = st[0:1] + st[1:2] + st[2:3]
            stat_s[2 * h + t, 1:2] = st[3:4] + st[4:5] + st[5:6]
            pos = z * (2 * TILE) + t * TILE + cq * RUN + lane
            start = jnp.zeros_like(pos)
            for e in ends:
                start = jnp.where(pos >= e, e, start)
            start_s[2 * h + t, 0:1] = start

    def first_start(pos):
        s = jnp.int32(0)
        for e in ends:
            s = jnp.where(e <= pos, e, s)
        return s

    row = lax.broadcasted_iota(jnp.int32, (ROWS, 1), 0)

    def slot_step(s, carry):
        for h, ref in enumerate((own_ref, other_ref)):
            cq = c if h == 0 else 1 - c

            def run_step(t, carry2):
                p0 = z * (2 * TILE) + t * TILE + cq * RUN
                s0 = first_start(p0)
                bases = []
                for half in range(2):
                    zk = base_s[2 * s + half]
                    ck = jnp.where((half == 0) | (s == 0), c, 1 - c)
                    b = zk * (2 * TILE) + ck * RUN + in_plane
                    ok = allow_ref[2 * z + t, jnp.maximum(2 * zk + yh, 0)] == 1
                    live = ok & (zk >= 0) & (b <= p0 + RUN - 1) & (b + ROWS - 1 >= s0)
                    bases.append((live, b))

                @pl.when(bases[0][0] | bases[1][0])
                def _unit():
                    k = k_s[s]
                    v = v_s[s]
                    kt = kt_s[s]
                    key = jnp.concatenate(
                        [jnp.where(live, b, FAR) + row for live, b in bases], axis=0
                    )
                    dk = jnp.zeros((CHUNK, WIDTH), jnp.float32)
                    dv = jnp.zeros((CHUNK, WIDTH), jnp.float32)
                    for n in range(RUN // CHUNK):
                        cols = slice(n * CHUNK, (n + 1) * CHUNK)
                        q = ref[pl.ds(8 * t + 2 * n, 2), 0:128, :].reshape(CHUNK, WIDTH)
                        g = ref[pl.ds(8 * t + 2 * n, 2), 128:256, :].reshape(CHUNK, WIDTH)
                        lse2 = stat_s[2 * h + t, 0:1, cols]
                        delta = stat_s[2 * h + t, 1:2, cols]
                        start = start_s[2 * h + t, 0:1, cols]
                        pos = p0 + lane[:, cols]
                        sc = lax.dot_general(
                            k, q, (((1,), (1,)), ((), ())), preferred_element_type=jnp.float32
                        )
                        dp = lax.dot_general(
                            v, g, (((1,), (1,)), ((), ())), preferred_element_type=jnp.float32
                        )
                        vis = (key >= start) & (key <= pos)
                        p = jnp.where(vis, jnp.exp2(sc * (SCALE * LOG2E) - lse2), 0.0)
                        pb = p.astype(jnp.bfloat16)
                        ds = (p * (dp - delta)).astype(jnp.bfloat16)
                        dv = dv + jnp.dot(pb, g, preferred_element_type=jnp.float32)
                        dk = dk + jnp.dot(ds, q, preferred_element_type=jnp.float32)
                        dqt_acc[2 * h + t, :, cols] += jnp.dot(
                            kt, ds, preferred_element_type=jnp.float32
                        )
                    dk_acc[s] += dk
                    dv_acc[s] += dv

                return carry2

            lax.fori_loop(0, 2, run_step, 0)
        return carry

    lax.fori_loop(0, 4, slot_step, 0)

    for h, out in enumerate((dqo_ref, dqx_ref)):
        for t in range(2):
            out[8 * t : 8 * t + 8] = (
                dqt_acc[2 * h + t].T.astype(jnp.bfloat16).reshape(8, ROWS, WIDTH)
            )
    for half, out in enumerate((d0_ref, d4_ref)):
        out[0:128] = dk_acc[0, half * ROWS : (half + 1) * ROWS].astype(jnp.bfloat16)
        out[128:256] = dv_acc[0, half * ROWS : (half + 1) * ROWS].astype(jnp.bfloat16)
    for out, s in ((d1_ref, 1), (d2_ref, 2), (d3_ref, 3)):
        for half in range(2):
            out[half, 0:128] = dk_acc[s, half * ROWS : (half + 1) * ROWS].astype(jnp.bfloat16)
            out[half, 128:256] = dv_acc[s, half * ROWS : (half + 1) * ROWS].astype(jnp.bfloat16)


def grads(where, doc_lengths, tile_allowed, own, other, kv0, kv4, kv1, kv2, kv3):
    smem = pl.BlockSpec(memory_space=pltpu.SMEM)
    vmem = pl.BlockSpec(memory_space=pltpu.VMEM)
    bf, f32 = jnp.bfloat16, jnp.float32
    one = jax.ShapeDtypeStruct((2 * ROWS, WIDTH), bf)
    two = jax.ShapeDtypeStruct((2, 2 * ROWS, WIDTH), bf)
    dq = jax.ShapeDtypeStruct((16, ROWS, WIDTH), bf)
    return pl.pallas_call(
        grad_kernel,
        out_shape=(dq, dq, one, one, two, two, two),
        in_specs=[smem, smem, smem] + [vmem] * 7,
        out_specs=(vmem,) * 7,
        scratch_shapes=[
            pltpu.VMEM((4, CHUNK, WIDTH), bf),
            pltpu.VMEM((4, CHUNK, WIDTH), bf),
            pltpu.VMEM((4, WIDTH, CHUNK), bf),
            pltpu.VMEM((4, CHUNK, WIDTH), f32),
            pltpu.VMEM((4, CHUNK, WIDTH), f32),
            pltpu.VMEM((4, WIDTH, RUN), f32),
            pltpu.VMEM((4, 8, RUN), f32),
            pltpu.VMEM((4, 8, RUN), jnp.int32),
            pltpu.SMEM((8,), jnp.int32),
        ],
        compiler_params=pltpu.CompilerParams(vmem_limit_bytes=32 * 1024 * 1024),
    )(where, doc_lengths, tile_allowed, own, other, kv0, kv4, kv1, kv2, kv3)


def on_device(
    queries, key_rows, value_rows, outputs, out_grad, log_sums, doc_lengths, tile_allowed
):
    z, yh, c = lax.axis_index("z"), lax.axis_index("yh"), lax.axis_index("c")
    koff = (lax.axis_index("x") * 2 + lax.axis_index("yl")) * ROWS
    where = jnp.stack([z, yh, c, koff]).astype(jnp.int32)
    swap = [(0, 1), (1, 0)]

    def along_z(x, k, both_ways=True, back=False):
        return lax.ppermute(x, AXES, pairs_along_z(k, both_ways, back))

    packed = pack(queries, out_grad, outputs, log_sums.reshape(1, ROWS))
    own = lax.all_to_all(packed, PLANE, 0, 0, tiled=True)

    kv0 = jnp.concatenate([key_rows, value_rows], axis=0)
    kv_pair = jnp.stack([kv0, lax.ppermute(kv0, "c", swap)])
    kv1, kv2, kv3 = (along_z(kv_pair, k) for k in (1, 2, 3))
    kv4 = along_z(kv0, 4, both_ways=False)
    other = lax.ppermute(own, "c", swap)

    dq_own, dq_other, d0, d4, d1, d2, d3 = grads(
        where, doc_lengths, tile_allowed, own, other, kv0, kv4, kv1, kv2, kv3
    )
    f32 = jnp.float32
    dq_in = lax.ppermute(dq_other, "c", swap)
    e1, e2, e3 = (along_z(d, k, back=True) for k, d in ((1, d1), (2, d2), (3, d3)))
    e4 = along_z(d4, 4, both_ways=False, back=True)
    dq_pair = (dq_own.astype(f32) + dq_in.astype(f32)).astype(jnp.bfloat16)
    dq_all = lax.all_to_all(dq_pair, PLANE, 0, 0, tiled=True)
    back = e1.astype(f32) + e2.astype(f32) + e3.astype(f32)
    from_core = lax.ppermute(back[1].astype(jnp.bfloat16), "c", swap)
    dkv = back[0] + e4.astype(f32) + d0.astype(f32) + from_core.astype(f32)
    query_grad = (jnp.sum(dq_all.astype(f32), axis=0) * SCALE).astype(jnp.bfloat16)
    key_grad = (dkv[:ROWS] * SCALE).astype(jnp.bfloat16)
    value_grad = dkv[ROWS:].astype(jnp.bfloat16)
    return query_grad, key_grad, value_grad


def solution(mesh):
    fine = Mesh(mesh.devices.reshape(SIZES), AXES)
    rows, vec = P(AXES, None), P(AXES)
    return jax.shard_map(
        on_device,
        mesh=fine,
        in_specs=(rows, rows, rows, rows, rows, vec, P(), P()),
        out_specs=(rows, rows, rows),
        check_vma=False,
    )
```

```python
import math

import jax
import jax.numpy as jnp
import numpy as np
from jax import lax
from jax.experimental import pallas as pl
from jax.experimental.pallas import tpu as pltpu
from jax.sharding import Mesh, PartitionSpec as P

AXES = ("z", "yh", "c", "x", "yl")
SIZES = (8, 2, 2, 4, 2)
PLANE = ("yh", "x", "yl")
ROWS = 128
WIDTH = 128
NDOCS = 16
TILE = 2048
RUN = 1024
CHUNK = 256
PACK = 272
LOG2E = math.log2(math.e)
SCALE = 128.0 ** -0.5
BF = jnp.bfloat16
F32 = jnp.float32
ONE = jax.ShapeDtypeStruct((2 * ROWS, WIDTH), BF)
TWO = jax.ShapeDtypeStruct((2, 2 * ROWS, WIDTH), BF)


def pairs_along_z(k, both_ways, back):
    pairs = []
    for i in range(256):
        z, yh, c, x, yl = (int(v) for v in np.unravel_index(i, SIZES))
        t = z - k + 8 if both_ways and c == 1 else z + k
        if z < t < 8:
            j = int(np.ravel_multi_index((t, yh, c, x, yl), SIZES))
            pairs.append((j, i) if back else (i, j))
    return pairs


def call(body, out_shape, *args, smem=0, scratch=()):
    specs = [pl.BlockSpec(memory_space=pltpu.SMEM)] * smem
    specs += [pl.BlockSpec(memory_space=pltpu.VMEM)] * (len(args) - smem)
    return pl.pallas_call(
        body,
        out_shape=out_shape,
        in_specs=specs,
        scratch_shapes=scratch,
        compiler_params=pltpu.CompilerParams(vmem_limit_bytes=32 * 1024 * 1024),
    )(*args)


def split3(x):
    a = x.astype(BF)
    r = x - a.astype(F32)
    b = r.astype(BF)
    c = (r - b.astype(F32)).astype(BF)
    return a, b, c


def pack_kernel(q_ref, g_ref, o_ref, lse_ref, out_ref):
    prod = g_ref[...].astype(F32) * o_ref[...].astype(F32)
    delta = jnp.sum(prod.T, axis=0, keepdims=True)
    lse2 = lse_ref[...] * LOG2E
    parts = split3(lse2) + split3(delta)
    stats = jnp.concatenate(
        [p.astype(F32) for p in parts] + [jnp.zeros((10, ROWS), F32)], axis=0
    ).astype(BF)
    for n in range(16):
        out_ref[n, 0:128] = q_ref[...]
        out_ref[n, 128:256] = g_ref[...]
        out_ref[n, 256:272] = stats


def grad_kernel(
    where_ref, len_ref, allow_ref, qg_ref,
    own_ref, own_x_ref, m1_ref, m2_ref, m3_ref, m4_ref, x1_ref, x2_ref, x3_ref, x4_ref,
    dq_ref, d0_ref, d1_ref, d2_ref, d3_ref, d4_ref, dx_ref,
    k_s, v_s, d_s, dk_acc, dv_acc, dqt_acc, stat_s, start_s, zk_s, ck_s,
):
    z, yh, c, koff = where_ref[0], where_ref[1], where_ref[2], where_ref[3]
    ends = []
    total = jnp.int32(0)
    for d in range(NDOCS):
        total = total + len_ref[d]
        ends.append(total)

    slots = (
        ((own_ref, None), (own_x_ref, None)),
        ((m1_ref, 0), (m1_ref, 1)),
        ((m2_ref, 0), (m2_ref, 1)),
        ((m3_ref, 0), (m3_ref, 1)),
        ((m4_ref, None), (x4_ref, None)),
        ((x1_ref, 0), (x1_ref, 1)),
        ((x2_ref, 0), (x2_ref, 1)),
        ((x3_ref, 0), (x3_ref, 1)),
    )
    for s, halves in enumerate(slots):
        for half, (ref, i) in enumerate(halves):
            rows = slice(half * ROWS, (half + 1) * ROWS)
            k_s[s, rows] = ref[0:128] if i is None else ref[i, 0:128]
            v_s[s, rows] = ref[128:256] if i is None else ref[i, 128:256]
    zk_s[0] = z
    zk_s[4] = z - 4
    for k in range(1, 4):
        zk_s[k] = jnp.where(c == 0, z - k, z + k - 8)
        zk_s[4 + k] = jnp.where(c == 0, z + k - 8, z - k)
    for s in range(8):
        ck_s[s] = c if s < 5 else 1 - c
    dqt_acc[...] = jnp.zeros_like(dqt_acc)

    lane = lax.broadcasted_iota(jnp.int32, (1, RUN), 1)
    for t in range(2):
        st = jnp.concatenate(
            [qg_ref[8 * t + n, 256:272].astype(F32) for n in range(8)], axis=1
        )
        stat_s[t, 0:1] = st[0:1] + st[1:2] + st[2:3]
        stat_s[t, 1:2] = st[3:4] + st[4:5] + st[5:6]
        pos = z * (2 * TILE) + t * TILE + c * RUN + lane
        start = jnp.zeros_like(pos)
        for e in ends:
            start = jnp.where(pos >= e, e, start)
        start_s[t, 0:1] = start

    first = []
    for t in range(2):
        p0 = z * (2 * TILE) + t * TILE + c * RUN
        s0 = jnp.int32(0)
        for e in ends:
            s0 = jnp.where(e <= p0, e, s0)
        first.append((p0, s0))

    row = lax.broadcasted_iota(jnp.int32, (ROWS, 1), 0)

    def slot_step(s, carry):
        zk, ck = zk_s[s], ck_s[s]
        b0 = zk * (2 * TILE) + yh * TILE + ck * RUN + koff
        b1 = zk * (2 * TILE) + yh * TILE + (1 - ck) * RUN + koff
        low, high = jnp.minimum(b0, b1), jnp.maximum(b0, b1)
        dk_acc[...] = jnp.zeros_like(dk_acc)
        dv_acc[...] = jnp.zeros_like(dv_acc)
        for t in range(2):
            p0, s0 = first[t]
            ok = allow_ref[2 * z + t, jnp.maximum(2 * zk + yh, 0)] == 1

            @pl.when(ok & (zk >= 0) & (low <= p0 + RUN - 1) & (high + ROWS - 1 >= s0))
            def _unit():
                k = k_s[s]
                v = v_s[s]
                kt = k.T
                key = jnp.concatenate([b0 + row, b1 + row], axis=0)
                dk = dk_acc[...]
                dv = dv_acc[...]
                for n in range(RUN // CHUNK):
                    cols = slice(n * CHUNK, (n + 1) * CHUNK)
                    blk = 8 * t + 2 * n
                    q = qg_ref[blk : blk + 2, 0:128, :].reshape(CHUNK, WIDTH)
                    g = qg_ref[blk : blk + 2, 128:256, :].reshape(CHUNK, WIDTH)
                    lse2 = stat_s[t, 0:1, cols]
                    delta = stat_s[t, 1:2, cols]
                    sc = lax.dot_general(
                        k, q, (((1,), (1,)), ((), ())), preferred_element_type=F32
                    )
                    dp = lax.dot_general(
                        v, g, (((1,), (1,)), ((), ())), preferred_element_type=F32
                    )
                    vis = (key >= start_s[t, 0:1, cols]) & (key <= p0 + lane[:, cols])
                    p = jnp.where(vis, jnp.exp2(sc * (SCALE * LOG2E) - lse2), 0.0)
                    pb = p.astype(BF)
                    ds = (p * (dp - delta)).astype(BF)
                    dv = dv + jnp.dot(pb, g, preferred_element_type=F32)
                    dk = dk + jnp.dot(ds, q, preferred_element_type=F32)
                    dqt_acc[t, :, cols] += jnp.dot(kt, ds, preferred_element_type=F32)
                dk_acc[...] = dk
                dv_acc[...] = dv

        for half in range(2):
            rows = slice(half * ROWS, (half + 1) * ROWS)
            d_s[2 * s + half, 0:128] = dk_acc[rows].astype(BF)
            d_s[2 * s + half, 128:256] = dv_acc[rows].astype(BF)
        return carry

    lax.fori_loop(0, 8, slot_step, 0)

    for t in range(2):
        for n in range(8):
            dq_ref[8 * t + n] = dqt_acc[t, :, n * ROWS : (n + 1) * ROWS].astype(BF)
    d0_ref[...] = d_s[0]
    d4_ref[...] = d_s[8]
    for k, out in enumerate((d1_ref, d2_ref, d3_ref)):
        out[...] = d_s[2 + 2 * k : 4 + 2 * k]
    dx_ref[0:6] = d_s[10:16]
    dx_ref[6] = d_s[1]
    dx_ref[7] = d_s[9]


def grads(*args):
    return call(
        grad_kernel,
        (
            jax.ShapeDtypeStruct((16, WIDTH, ROWS), BF),
            ONE, TWO, TWO, TWO, ONE,
            jax.ShapeDtypeStruct((8, 2 * ROWS, WIDTH), BF),
        ),
        *args,
        smem=3,
        scratch=[
            pltpu.VMEM((8, CHUNK, WIDTH), BF),
            pltpu.VMEM((8, CHUNK, WIDTH), BF),
            pltpu.VMEM((16, 2 * ROWS, WIDTH), BF),
            pltpu.VMEM((CHUNK, WIDTH), F32),
            pltpu.VMEM((CHUNK, WIDTH), F32),
            pltpu.VMEM((2, WIDTH, RUN), F32),
            pltpu.VMEM((2, 8, RUN), F32),
            pltpu.VMEM((2, 8, RUN), jnp.int32),
            pltpu.SMEM((8,), jnp.int32),
            pltpu.SMEM((8,), jnp.int32),
        ],
    )


def pair_kernel(d0, d1, d2, d3, d4, got, s0, s1, s2, s3, s4):
    for k, (a, out) in enumerate(((d1, s1), (d2, s2), (d3, s3))):
        out[...] = (a[...].astype(F32) + got[2 * k : 2 * k + 2].astype(F32)).astype(BF)
    s0[...] = (d0[...].astype(F32) + got[6].astype(F32)).astype(BF)
    s4[...] = (d4[...].astype(F32) + got[7].astype(F32)).astype(BF)


def column_kernel(s0, e1, e2, e3, e4, keep, send):
    total = e1[...].astype(F32) + e2[...].astype(F32) + e3[...].astype(F32)
    keep[...] = total[0] + e4[...].astype(F32) + s0[...].astype(F32)
    send[...] = total[1].astype(BF)


def last_kernel(dq_all, keep, got, dq_ref, dk_ref, dv_ref):
    dq = dq_all[0].astype(F32)
    for n in range(1, 16):
        dq = dq + dq_all[n].astype(F32)
    dq_ref[...] = (dq.T * SCALE).astype(BF)
    dkv = keep[...] + got[...].astype(F32)
    dk_ref[...] = (dkv[:ROWS] * SCALE).astype(BF)
    dv_ref[...] = dkv[ROWS:].astype(BF)


def on_device(
    queries, key_rows, value_rows, outputs, out_grad, log_sums, doc_lengths, tile_allowed
):
    z, yh, c = lax.axis_index("z"), lax.axis_index("yh"), lax.axis_index("c")
    koff = (lax.axis_index("x") * 2 + lax.axis_index("yl")) * ROWS
    where = jnp.stack([z, yh, c, koff]).astype(jnp.int32)

    def swap(x):
        return lax.ppermute(x, "c", [(0, 1), (1, 0)])

    def along_z(x, k, both_ways=True, back=False):
        return lax.ppermute(x, AXES, pairs_along_z(k, both_ways, back))

    packed = call(
        pack_kernel,
        jax.ShapeDtypeStruct((16, PACK, WIDTH), BF),
        queries, out_grad, outputs, log_sums.reshape(1, ROWS),
    )
    qg = lax.all_to_all(packed, PLANE, 0, 0, tiled=True)

    own = jnp.concatenate([key_rows, value_rows], axis=0)
    own_x = swap(own)
    both = jnp.stack([own, own_x])
    mine = [along_z(both, k) for k in (1, 2, 3)] + [along_z(own, 4, both_ways=False)]
    theirs = [swap(m) for m in mine]

    dq, d0, d1, d2, d3, d4, dx = grads(
        where, doc_lengths, tile_allowed, qg, own, own_x, *mine, *theirs
    )
    dq_all = lax.all_to_all(dq, PLANE, 0, 0, tiled=True)
    s0, s1, s2, s3, s4 = call(
        pair_kernel, (ONE, TWO, TWO, TWO, ONE), d0, d1, d2, d3, d4, swap(dx)
    )
    e1, e2, e3 = (along_z(s, k, back=True) for k, s in ((1, s1), (2, s2), (3, s3)))
    e4 = along_z(s4, 4, both_ways=False, back=True)
    keep, send = call(
        column_kernel,
        (jax.ShapeDtypeStruct((2 * ROWS, WIDTH), F32), ONE),
        s0, e1, e2, e3, e4,
    )
    out = jax.ShapeDtypeStruct((ROWS, WIDTH), BF)
    return call(last_kernel, (out, out, out), dq_all, keep, swap(send))


def solution(mesh):
    fine = Mesh(mesh.devices.reshape(SIZES), AXES)
    rows, vec = P(AXES, None), P(AXES)
    return jax.shard_map(
        on_device,
        mesh=fine,
        in_specs=(rows, rows, rows, rows, rows, vec, P(), P()),
        out_specs=(rows, rows, rows),
        check_vma=False,
    )
```

```python
import math

import jax
import jax.numpy as jnp
import numpy as np
from jax import lax
from jax.experimental import pallas as pl
from jax.experimental.pallas import tpu as pltpu
from jax.sharding import Mesh, PartitionSpec as P

AXES = ("z", "yh", "c", "x", "yl")
SIZES = (8, 2, 2, 4, 2)
PLANE = ("yh", "x", "yl")
ROWS = 128
WIDTH = 128
NDOCS = 16
TILE = 2048
RUN = 1024
CHUNK = 256
PACK = 272
LOG2E = math.log2(math.e)
SCALE = 128.0 ** -0.5
BF = jnp.bfloat16
F32 = jnp.float32
ONE = jax.ShapeDtypeStruct((WIDTH, ROWS), BF)
TWO = jax.ShapeDtypeStruct((2, WIDTH, ROWS), BF)
KV = jax.ShapeDtypeStruct((16, 2 * ROWS, WIDTH), BF)


def pairs_along_z(k, both_ways, back):
    pairs = []
    for i in range(256):
        z, yh, c, x, yl = (int(v) for v in np.unravel_index(i, SIZES))
        t = z - k + 8 if both_ways and c == 1 else z + k
        if z < t < 8:
            j = int(np.ravel_multi_index((t, yh, c, x, yl), SIZES))
            pairs.append((j, i) if back else (i, j))
    return pairs


def call(body, out_shape, *args, smem=0, scratch=()):
    specs = [pl.BlockSpec(memory_space=pltpu.SMEM)] * smem
    specs += [pl.BlockSpec(memory_space=pltpu.VMEM)] * (len(args) - smem)
    return pl.pallas_call(
        body,
        out_shape=out_shape,
        in_specs=specs,
        scratch_shapes=scratch,
        compiler_params=pltpu.CompilerParams(vmem_limit_bytes=32 * 1024 * 1024),
    )(*args)


def split3(x):
    a = x.astype(BF)
    r = x - a.astype(F32)
    b = r.astype(BF)
    c = (r - b.astype(F32)).astype(BF)
    return a, b, c


def prep_kernel(
    q_hbm, g_hbm, o_hbm, lse_hbm, k_hbm, v_hbm, pack_ref, kv_hbm, o_s, lse_s, kv_s, sems
):
    loads = [
        pltpu.make_async_copy(k_hbm, kv_s.at[0:128], sems.at[0]),
        pltpu.make_async_copy(v_hbm, kv_s.at[128:256], sems.at[1]),
        pltpu.make_async_copy(g_hbm, pack_ref.at[128:256], sems.at[2]),
        pltpu.make_async_copy(o_hbm, o_s, sems.at[3]),
        pltpu.make_async_copy(lse_hbm, lse_s, sems.at[4]),
        pltpu.make_async_copy(q_hbm, pack_ref.at[0:128], sems.at[5]),
    ]
    for copy in loads:
        copy.start()
    loads[0].wait()
    loads[1].wait()
    stores = [pltpu.make_async_copy(kv_s, kv_hbm.at[n], sems.at[6 + n]) for n in range(16)]
    for copy in stores:
        copy.start()
    loads[2].wait()
    loads[3].wait()
    loads[4].wait()
    prod = pack_ref[128:256].astype(F32) * o_s[...].astype(F32)
    delta = jnp.sum(prod.T, axis=0, keepdims=True)
    lse2 = lse_s[...] * LOG2E
    parts = split3(lse2) + split3(delta)
    stats = [p.astype(F32) for p in parts] + [jnp.zeros((10, ROWS), F32)]
    pack_ref[256:272] = jnp.concatenate(stats, axis=0).astype(BF)
    loads[5].wait()
    for copy in stores:
        copy.wait()


def prep(*args):
    anywhere = pl.BlockSpec(memory_space=pl.ANY)
    return pl.pallas_call(
        prep_kernel,
        out_shape=(jax.ShapeDtypeStruct((PACK, WIDTH), BF), KV),
        in_specs=[anywhere] * 6,
        out_specs=(pl.BlockSpec(memory_space=pltpu.VMEM), anywhere),
        scratch_shapes=[
            pltpu.VMEM((ROWS, WIDTH), BF),
            pltpu.VMEM((1, ROWS), F32),
            pltpu.VMEM((2 * ROWS, WIDTH), BF),
            pltpu.SemaphoreType.DMA((22,)),
        ],
    )(*args)


def grad_kernel(
    where_ref, len_ref, allow_ref, kv_ref,
    own_ref, own_x_ref, m1_ref, m2_ref, m3_ref, m4_ref, x1_ref, x2_ref, x3_ref, x4_ref,
    dkv_ref, d0_ref, d1_ref, d2_ref, d3_ref, d4_ref, dx_ref,
    q_s, g_s, st_s, d_s, kt_s, dk_acc, dv_acc, dqt_s, zq_s, cq_s,
):
    z, yh, c, off = where_ref[0], where_ref[1], where_ref[2], where_ref[3]
    ends = []
    total = jnp.int32(0)
    for d in range(NDOCS):
        total = total + len_ref[d]
        ends.append(total)

    slots = (
        ((own_ref, None), (own_x_ref, None)),
        ((m1_ref, 0), (m1_ref, 1)),
        ((m2_ref, 0), (m2_ref, 1)),
        ((m3_ref, 0), (m3_ref, 1)),
        ((m4_ref, None), (x4_ref, None)),
        ((x1_ref, 0), (x1_ref, 1)),
        ((x2_ref, 0), (x2_ref, 1)),
        ((x3_ref, 0), (x3_ref, 1)),
    )
    for s, halves in enumerate(slots):
        for half, (ref, i) in enumerate(halves):
            rows = slice(half * ROWS, (half + 1) * ROWS)
            q_s[s, rows] = ref[0:128] if i is None else ref[i, 0:128]
            g_s[s, rows] = ref[128:256] if i is None else ref[i, 128:256]
            st_s[s, :, rows] = (ref[256:272] if i is None else ref[i, 256:272]).astype(F32)
    zq_s[0] = z
    zq_s[4] = z + 4
    for k in range(1, 4):
        zq_s[k] = jnp.where(c == 0, z + k, z - k + 8)
        zq_s[4 + k] = jnp.where(c == 0, z - k + 8, z + k)
    for s in range(8):
        cq_s[s] = c if s < 5 else 1 - c
    for t in range(2):
        kt_s[t] = kv_ref[8 * t : 8 * t + 8, 0:128, :].reshape(RUN, WIDTH).T
    dk_acc[...] = jnp.zeros_like(dk_acc)
    dv_acc[...] = jnp.zeros_like(dv_acc)

    lane = lax.broadcasted_iota(jnp.int32, (1, 2 * ROWS), 1)
    row = lax.broadcasted_iota(jnp.int32, (CHUNK, 1), 0)

    def slot_step(s, carry):
        zq, cq = zq_s[s], cq_s[s]
        p0 = zq * (2 * TILE) + yh * TILE + cq * RUN + off
        p1 = zq * (2 * TILE) + yh * TILE + (1 - cq) * RUN + off
        low, high = jnp.minimum(p0, p1), jnp.maximum(p0, p1)
        low_start = jnp.int32(0)
        for e in ends:
            low_start = jnp.where(e <= low, e, low_start)
        dqt_s[...] = jnp.zeros_like(dqt_s)
        for t in range(2):
            b = z * (2 * TILE) + t * TILE + c * RUN
            ok = allow_ref[jnp.minimum(2 * zq + yh, 15), 2 * z + t] == 1

            @pl.when(ok & (zq < 8) & (b <= high + ROWS - 1) & (b + RUN - 1 >= low_start))
            def _unit():
                q = q_s[s]
                g = g_s[s]
                st = st_s[s]
                lse2 = st[0:1] + st[1:2] + st[2:3]
                delta = st[3:4] + st[4:5] + st[5:6]
                pos = jnp.where(lane < ROWS, p0 + lane, p1 - ROWS + lane)
                start = jnp.zeros_like(pos)
                for e in ends:
                    start = jnp.where(pos >= e, e, start)
                dqt = dqt_s[...]
                for n in range(RUN // CHUNK):
                    blk = 8 * t + 2 * n
                    k = kv_ref[blk : blk + 2, 0:128, :].reshape(CHUNK, WIDTH)
                    v = kv_ref[blk : blk + 2, 128:256, :].reshape(CHUNK, WIDTH)
                    sc = lax.dot_general(
                        k, q, (((1,), (1,)), ((), ())), preferred_element_type=F32
                    )
                    dp = lax.dot_general(
                        v, g, (((1,), (1,)), ((), ())), preferred_element_type=F32
                    )
                    key = b + n * CHUNK + row
                    vis = (key >= start) & (key <= pos)
                    p = jnp.where(vis, jnp.exp2(sc * (SCALE * LOG2E) - lse2), 0.0)
                    pb = p.astype(BF)
                    ds = (p * (dp - delta)).astype(BF)
                    rows = slice(t * RUN + n * CHUNK, t * RUN + (n + 1) * CHUNK)
                    dv_acc[rows] += jnp.dot(pb, g, preferred_element_type=F32)
                    dk_acc[rows] += jnp.dot(ds, q, preferred_element_type=F32)
                    dqt = dqt + jnp.dot(
                        kt_s[t, :, n * CHUNK : (n + 1) * CHUNK], ds, preferred_element_type=F32
                    )
                dqt_s[...] = dqt

        for half in range(2):
            d_s[2 * s + half] = dqt_s[:, half * ROWS : (half + 1) * ROWS].astype(BF)
        return carry

    lax.fori_loop(0, 8, slot_step, 0)

    for n in range(16):
        rows = slice(n * ROWS, (n + 1) * ROWS)
        dkv_ref[n, 0:128] = dk_acc[rows].astype(BF)
        dkv_ref[n, 128:256] = dv_acc[rows].astype(BF)
    d0_ref[...] = d_s[0]
    d4_ref[...] = d_s[8]
    for k, out in enumerate((d1_ref, d2_ref, d3_ref)):
        out[...] = d_s[2 + 2 * k : 4 + 2 * k]
    dx_ref[0:6] = d_s[10:16]
    dx_ref[6] = d_s[1]
    dx_ref[7] = d_s[9]


def grads(*args):
    return call(
        grad_kernel,
        (KV, ONE, TWO, TWO, TWO, ONE, jax.ShapeDtypeStruct((8, WIDTH, ROWS), BF)),
        *args,
        smem=3,
        scratch=[
            pltpu.VMEM((8, 2 * ROWS, WIDTH), BF),
            pltpu.VMEM((8, 2 * ROWS, WIDTH), BF),
            pltpu.VMEM((8, 16, 2 * ROWS), F32),
            pltpu.VMEM((16, WIDTH, ROWS), BF),
            pltpu.VMEM((2, WIDTH, RUN), BF),
            pltpu.VMEM((2 * RUN, WIDTH), F32),
            pltpu.VMEM((2 * RUN, WIDTH), F32),
            pltpu.VMEM((WIDTH, 2 * ROWS), F32),
            pltpu.SMEM((8,), jnp.int32),
            pltpu.SMEM((8,), jnp.int32),
        ],
    )


def pair_kernel(d0, d1, d2, d3, d4, got, s0, s1, s2, s3, s4):
    for k, (a, out) in enumerate(((d1, s1), (d2, s2), (d3, s3))):
        out[...] = (a[...].astype(F32) + got[2 * k : 2 * k + 2].astype(F32)).astype(BF)
    s0[...] = (d0[...].astype(F32) + got[6].astype(F32)).astype(BF)
    s4[...] = (d4[...].astype(F32) + got[7].astype(F32)).astype(BF)


def column_kernel(s0, e1, e2, e3, e4, keep, send):
    total = e1[...].astype(F32) + e2[...].astype(F32) + e3[...].astype(F32)
    keep[...] = total[0] + e4[...].astype(F32) + s0[...].astype(F32)
    send[...] = total[1].astype(BF)


def last_kernel(dkv_all, keep, got, dq_ref, dk_ref, dv_ref):
    dkv = dkv_all[0].astype(F32)
    for n in range(1, 16):
        dkv = dkv + dkv_all[n].astype(F32)
    dk_ref[...] = (dkv[:ROWS] * SCALE).astype(BF)
    dv_ref[...] = dkv[ROWS:].astype(BF)
    dq_ref[...] = ((keep[...] + got[...].astype(F32)).T * SCALE).astype(BF)


def on_device(
    queries, key_rows, value_rows, outputs, out_grad, log_sums, doc_lengths, tile_allowed
):
    z, yh, c = lax.axis_index("z"), lax.axis_index("yh"), lax.axis_index("c")
    off = (lax.axis_index("x") * 2 + lax.axis_index("yl")) * ROWS
    where = jnp.stack([z, yh, c, off]).astype(jnp.int32)

    def swap(x):
        return lax.ppermute(x, "c", [(0, 1), (1, 0)])

    def along_z(x, k, both_ways=True, back=False):
        return lax.ppermute(x, AXES, pairs_along_z(k, both_ways, back))

    own, kv_out = prep(
        queries, out_grad, outputs, log_sums.reshape(1, ROWS), key_rows, value_rows
    )
    kv = lax.all_to_all(kv_out, PLANE, 0, 0, tiled=True)
    own_x = swap(own)
    both = jnp.stack([own, own_x])
    mine = [along_z(both, k, back=True) for k in (1, 2, 3)]
    mine.append(along_z(own, 4, both_ways=False, back=True))
    theirs = [swap(m) for m in mine]

    dkv, d0, d1, d2, d3, d4, dx = grads(
        where, doc_lengths, tile_allowed, kv, own, own_x, *mine, *theirs
    )
    dkv_all = lax.all_to_all(dkv, PLANE, 0, 0, tiled=True)
    s0, s1, s2, s3, s4 = call(
        pair_kernel, (ONE, TWO, TWO, TWO, ONE), d0, d1, d2, d3, d4, swap(dx)
    )
    e1, e2, e3 = (along_z(s, k) for k, s in ((1, s1), (2, s2), (3, s3)))
    e4 = along_z(s4, 4, both_ways=False)
    keep, send = call(
        column_kernel,
        (jax.ShapeDtypeStruct((WIDTH, ROWS), F32), ONE),
        s0, e1, e2, e3, e4,
    )
    out = jax.ShapeDtypeStruct((ROWS, WIDTH), BF)
    return call(last_kernel, (out, out, out), dkv_all, keep, swap(send))


def solution(mesh):
    fine = Mesh(mesh.devices.reshape(SIZES), AXES)
    rows, vec = P(AXES, None), P(AXES)
    return jax.shard_map(
        on_device,
        mesh=fine,
        in_specs=(rows, rows, rows, rows, rows, vec, P(), P()),
        out_specs=(rows, rows, rows),
        check_vma=False,
    )
```

```python
import math

import jax
import jax.numpy as jnp
import numpy as np
from jax import lax
from jax.experimental import pallas as pl
from jax.experimental.pallas import tpu as pltpu
from jax.sharding import Mesh, PartitionSpec as P

AXES = ("z", "yh", "c", "x", "yl")
SIZES = (8, 2, 2, 4, 2)
PLANE = ("yh", "x", "yl")
ROWS = 128
WIDTH = 128
NDOCS = 16
TILE = 2048
RUN = 1024
PACK = 272
LOG2E = math.log2(math.e)
SCALE = 128.0 ** -0.5
SLOTS_COST = pl.CostEstimate(flops=8000000000, bytes_accessed=4 << 20, transcendentals=0)
PAIR_COST = pl.CostEstimate(flops=9000000000, bytes_accessed=1 << 20, transcendentals=0)
BF = jnp.bfloat16
F32 = jnp.float32
ONE = jax.ShapeDtypeStruct((WIDTH, ROWS), BF)
TWO = jax.ShapeDtypeStruct((2, WIDTH, ROWS), BF)
KV = jax.ShapeDtypeStruct((16, 2 * ROWS, WIDTH), BF)


def pairs_along_z(k, both_ways, back):
    pairs = []
    for i in range(256):
        z, yh, c, x, yl = (int(v) for v in np.unravel_index(i, SIZES))
        t = z - k + 8 if both_ways and c == 1 else z + k
        if z < t < 8:
            j = int(np.ravel_multi_index((t, yh, c, x, yl), SIZES))
            pairs.append((j, i) if back else (i, j))
    return pairs


def call(body, out_shape, *args, smem=0, scratch=(), cost=None, out_specs=None):
    specs = [pl.BlockSpec(memory_space=pltpu.SMEM)] * smem
    specs += [pl.BlockSpec(memory_space=pltpu.VMEM)] * (len(args) - smem)
    return pl.pallas_call(
        body,
        out_shape=out_shape,
        in_specs=specs,
        **({} if out_specs is None else {"out_specs": out_specs}),
        scratch_shapes=scratch,
        cost_estimate=cost,
        compiler_params=pltpu.CompilerParams(vmem_limit_bytes=32 * 1024 * 1024),
    )(*args)


def split3(x):
    a = x.astype(BF)
    r = x - a.astype(F32)
    b = r.astype(BF)
    c = (r - b.astype(F32)).astype(BF)
    return a, b, c


def prep_kernel(
    q_hbm, g_hbm, o_hbm, lse_hbm, k_hbm, v_hbm, pack_ref, kv_hbm, o_s, lse_s, kv_s, sems
):
    loads = [
        pltpu.make_async_copy(k_hbm, kv_s.at[0:128], sems.at[0]),
        pltpu.make_async_copy(v_hbm, kv_s.at[128:256], sems.at[1]),
        pltpu.make_async_copy(g_hbm, pack_ref.at[128:256], sems.at[2]),
        pltpu.make_async_copy(o_hbm, o_s, sems.at[3]),
        pltpu.make_async_copy(lse_hbm, lse_s, sems.at[4]),
        pltpu.make_async_copy(q_hbm, pack_ref.at[0:128], sems.at[5]),
    ]
    for copy in loads:
        copy.start()
    loads[0].wait()
    loads[1].wait()
    stores = [pltpu.make_async_copy(kv_s, kv_hbm.at[n], sems.at[6 + n]) for n in range(16)]
    for copy in stores:
        copy.start()
    loads[2].wait()
    loads[3].wait()
    loads[4].wait()
    prod = pack_ref[128:256].astype(F32) * o_s[...].astype(F32)
    delta = jnp.sum(prod.T, axis=0, keepdims=True)
    lse2 = lse_s[...] * LOG2E
    parts = split3(lse2) + split3(delta)
    stats = [p.astype(F32) for p in parts] + [jnp.zeros((10, ROWS), F32)]
    pack_ref[256:272] = jnp.concatenate(stats, axis=0).astype(BF)
    loads[5].wait()
    for copy in stores:
        copy.wait()


def prep(*args):
    anywhere = pl.BlockSpec(memory_space=pl.ANY)
    return pl.pallas_call(
        prep_kernel,
        out_shape=(jax.ShapeDtypeStruct((PACK, WIDTH), BF), KV),
        in_specs=[anywhere] * 6,
        out_specs=(pl.BlockSpec(memory_space=pltpu.VMEM), anywhere),
        scratch_shapes=[
            pltpu.VMEM((ROWS, WIDTH), BF),
            pltpu.VMEM((1, ROWS), F32),
            pltpu.VMEM((2 * ROWS, WIDTH), BF),
            pltpu.SemaphoreType.DMA((22,)),
        ],
    )(*args)


def slot_of(s, z, c):
    k = jnp.where(s < 5, s, s - 4)
    near = jnp.where(s < 5, c == 0, c == 1)
    zq = jnp.where(near | (k == 0) | (k == 4), z + k, z - k + 8)
    return zq, jnp.where(s < 5, c, 1 - c)


def slots_kernel(
    where_ref, len_ref, allow_ref, own_ref, own_x_ref, m1_ref, m2_ref, m3_ref, m4_ref, x1_ref, x2_ref, x3_ref, x4_ref,
    q_ref, g_ref, st_ref, at_ref, live_ref,
):
    z, yh, c, off = (where_ref[i] for i in range(4))
    ends = []
    total = jnp.int32(0)
    for d in range(NDOCS):
        total = total + len_ref[d]
        ends.append(total)
    slots = (
        ((own_ref, None), (own_x_ref, None)),
        ((m1_ref, 0), (m1_ref, 1)),
        ((m2_ref, 0), (m2_ref, 1)),
        ((m3_ref, 0), (m3_ref, 1)),
        ((m4_ref, None), (x4_ref, None)),
        ((x1_ref, 0), (x1_ref, 1)),
        ((x2_ref, 0), (x2_ref, 1)),
        ((x3_ref, 0), (x3_ref, 1)),
    )
    lane = lax.broadcasted_iota(jnp.int32, (1, 2 * ROWS), 1)
    pos_all = []
    for s, halves in enumerate(slots):
        stats = []
        for half, (ref, i) in enumerate(halves):
            rows = slice(half * ROWS, (half + 1) * ROWS)
            q_ref[s, rows] = ref[0:128] if i is None else ref[i, 0:128]
            g_ref[s, rows] = ref[128:256] if i is None else ref[i, 128:256]
            stats.append((ref[256:272] if i is None else ref[i, 256:272]).astype(F32))
        st = jnp.concatenate(stats, axis=1)
        st_ref[s, 0:1] = st[0:1] + st[1:2] + st[2:3]
        st_ref[s, 1:2] = st[3:4] + st[4:5] + st[5:6]
        zq, cq = slot_of(jnp.int32(s), z, c)
        base = zq * (2 * TILE) + yh * TILE + off
        pos_all.append(
            jnp.where(lane < ROWS, base + cq * RUN + lane, base + (1 - cq) * RUN - ROWS + lane)
        )
    pos = jnp.concatenate(pos_all, axis=0)
    start = jnp.zeros_like(pos)
    for e in ends:
        start = jnp.where(pos >= e, e, start)
    for s in range(8):
        at_ref[s, 0:1] = start[s : s + 1]
        at_ref[s, 1:2] = pos[s : s + 1]
        zq, _ = slot_of(jnp.int32(s), z, c)
        low = zq * (2 * TILE) + yh * TILE + off
        low_start = jnp.int32(0)
        for e in ends:
            low_start = jnp.where(e <= low, e, low_start)
        for t in range(2):
            b = z * (2 * TILE) + t * TILE + c * RUN
            ok = allow_ref[jnp.minimum(2 * zq + yh, 15), 2 * z + t] == 1
            ok = ok & (zq < 8) & (b <= low + RUN + ROWS - 1) & (b + RUN - 1 >= low_start)
            live_ref[8 * t + s] = ok.astype(jnp.int32)
    live_ref[16] = z * (2 * TILE) + c * RUN


def slots(*args):
    block = jax.ShapeDtypeStruct((8, 2 * ROWS, WIDTH), BF)
    vmem = pl.BlockSpec(memory_space=pltpu.VMEM)
    return call(
        slots_kernel,
        (
            block,
            block,
            jax.ShapeDtypeStruct((8, 8, 2 * ROWS), F32),
            jax.ShapeDtypeStruct((8, 8, 2 * ROWS), jnp.int32),
            jax.ShapeDtypeStruct((32,), jnp.int32),
        ),
        *args,
        smem=3,
        cost=SLOTS_COST,
        out_specs=(vmem, vmem, vmem, vmem, pl.BlockSpec(memory_space=pltpu.SMEM)),
    )


def grad_kernel(
    live_ref, kv_ref, q_ref, g_ref, st_ref, at_ref,
    dkv_hbm, d0_ref, d1_ref, d2_ref, d3_ref, d4_ref, dx_ref,
    kt_s, dk_acc, dv_acc, dqt_s, out_s, sems,
):
    row = lax.broadcasted_iota(jnp.int32, (RUN, 1), 0)
    dqt_s[...] = jnp.zeros_like(dqt_s)
    stores = []
    for t in range(2):
        kt_s[...] = kv_ref[8 * t : 8 * t + 8, 0:128, :].reshape(RUN, WIDTH).T
        dk_acc[...] = jnp.zeros_like(dk_acc)
        dv_acc[...] = jnp.zeros_like(dv_acc)
        b = live_ref[16] + t * TILE

        def slot_step(s, carry):
            @pl.when(live_ref[8 * t + s] == 1)
            def _unit():
                q = q_ref[s]
                g = g_ref[s]
                lse2 = st_ref[s, 0:1]
                delta = st_ref[s, 1:2]
                start = at_ref[s, 0:1]
                pos = at_ref[s, 1:2]
                k = kv_ref[8 * t : 8 * t + 8, 0:128, :].reshape(RUN, WIDTH)
                v = kv_ref[8 * t : 8 * t + 8, 128:256, :].reshape(RUN, WIDTH)
                sc = lax.dot_general(k, q, (((1,), (1,)), ((), ())), preferred_element_type=F32)
                dp = lax.dot_general(v, g, (((1,), (1,)), ((), ())), preferred_element_type=F32)
                key = b + row
                vis = (key >= start) & (key <= pos)
                p = jnp.where(vis, jnp.exp2(sc * (SCALE * LOG2E) - lse2), 0.0)
                ds = (p * (dp - delta)).astype(BF)
                dv_acc[...] += jnp.dot(p.astype(BF), g, preferred_element_type=F32)
                dk_acc[...] += jnp.dot(ds, q, preferred_element_type=F32)
                dqt_s[s] += jnp.dot(kt_s[...], ds, preferred_element_type=F32)

            return carry

        lax.fori_loop(0, 8, slot_step, 0)
        for n in range(8):
            rows = slice(n * ROWS, (n + 1) * ROWS)
            out_s[8 * t + n, 0:128] = dk_acc[rows].astype(BF)
            out_s[8 * t + n, 128:256] = dv_acc[rows].astype(BF)
        part = pl.ds(8 * t, 8)
        stores.append(pltpu.make_async_copy(out_s.at[part], dkv_hbm.at[part], sems.at[t]))
        stores[t].start()

    def term(s, half):
        return dqt_s[s, :, half * ROWS : (half + 1) * ROWS].astype(BF)

    d0_ref[...] = term(0, 0)
    d4_ref[...] = term(4, 0)
    for k, out in enumerate((d1_ref, d2_ref, d3_ref)):
        for half in range(2):
            out[half] = term(k + 1, half)
            dx_ref[2 * k + half] = term(k + 5, half)
    dx_ref[6] = term(0, 1)
    dx_ref[7] = term(4, 1)
    for copy in stores:
        copy.wait()


def grads(*args):
    vmem = pl.BlockSpec(memory_space=pltpu.VMEM)
    return call(
        grad_kernel,
        (KV, ONE, TWO, TWO, TWO, ONE, jax.ShapeDtypeStruct((8, WIDTH, ROWS), BF)),
        *args,
        smem=1,
        out_specs=(pl.BlockSpec(memory_space=pl.ANY),) + (vmem,) * 6,
        scratch=[
            pltpu.VMEM((WIDTH, RUN), BF),
            pltpu.VMEM((RUN, WIDTH), F32),
            pltpu.VMEM((RUN, WIDTH), F32),
            pltpu.VMEM((8, WIDTH, 2 * ROWS), F32),
            pltpu.VMEM((16, 2 * ROWS, WIDTH), BF),
            pltpu.SemaphoreType.DMA((2,)),
        ],
    )


def pair_kernel(d0, d1, d2, d3, d4, got, s0, s1, s2, s3, s4):
    for k, (a, out) in enumerate(((d1, s1), (d2, s2), (d3, s3))):
        out[...] = (a[...].astype(F32) + got[2 * k : 2 * k + 2].astype(F32)).astype(BF)
    s0[...] = (d0[...].astype(F32) + got[6].astype(F32)).astype(BF)
    s4[...] = (d4[...].astype(F32) + got[7].astype(F32)).astype(BF)


def column_kernel(s0, e1, e2, e3, e4, keep, send):
    total = e1[...].astype(F32) + e2[...].astype(F32) + e3[...].astype(F32)
    keep[...] = total[0] + e4[...].astype(F32) + s0[...].astype(F32)
    send[...] = total[1].astype(BF)


def last_kernel(dkv_all, keep, got, dq_ref, dk_ref, dv_ref):
    dkv = dkv_all[0].astype(F32)
    for n in range(1, 16):
        dkv = dkv + dkv_all[n].astype(F32)
    dk_ref[...] = (dkv[:ROWS] * SCALE).astype(BF)
    dv_ref[...] = dkv[ROWS:].astype(BF)
    dq_ref[...] = ((keep[...] + got[...].astype(F32)).T * SCALE).astype(BF)


def on_device(
    queries, key_rows, value_rows, outputs, out_grad, log_sums, doc_lengths, tile_allowed
):
    z, yh, c = lax.axis_index("z"), lax.axis_index("yh"), lax.axis_index("c")
    off = (lax.axis_index("x") * 2 + lax.axis_index("yl")) * ROWS
    where = jnp.stack([z, yh, c, off]).astype(jnp.int32)

    def swap(x):
        return lax.ppermute(x, "c", [(0, 1), (1, 0)])

    def along_z(x, k, both_ways=True, back=False):
        return lax.ppermute(x, AXES, pairs_along_z(k, both_ways, back))

    own, kv_out = prep(
        queries, out_grad, outputs, log_sums.reshape(1, ROWS), key_rows, value_rows
    )
    kv = lax.all_to_all(kv_out, PLANE, 0, 0, tiled=True)
    own_x = swap(own)
    both = jnp.stack([own, own_x])
    mine = [along_z(both, k, back=True) for k in (1, 2, 3)]
    mine.append(along_z(own, 4, both_ways=False, back=True))
    theirs = [swap(m) for m in mine]

    q, g, stats, at, live = slots(
        where, doc_lengths, tile_allowed, own, own_x, *mine, *theirs
    )
    dkv, d0, d1, d2, d3, d4, dx = grads(live, kv, q, g, stats, at)
    dkv_all = lax.all_to_all(dkv, PLANE, 0, 0, tiled=True)
    s0, s1, s2, s3, s4 = call(
        pair_kernel, (ONE, TWO, TWO, TWO, ONE), d0, d1, d2, d3, d4, swap(dx), cost=PAIR_COST
    )
    e1, e2, e3 = (along_z(s, k) for k, s in ((1, s1), (2, s2), (3, s3)))
    e4 = along_z(s4, 4, both_ways=False)
    keep, send = call(
        column_kernel,
        (jax.ShapeDtypeStruct((WIDTH, ROWS), F32), ONE),
        s0, e1, e2, e3, e4,
    )
    out = jax.ShapeDtypeStruct((ROWS, WIDTH), BF)
    return call(last_kernel, (out, out, out), dkv_all, keep, swap(send))


def solution(mesh):
    fine = Mesh(mesh.devices.reshape(SIZES), AXES)
    rows, vec = P(AXES, None), P(AXES)
    return jax.shard_map(
        on_device,
        mesh=fine,
        in_specs=(rows, rows, rows, rows, rows, vec, P(), P()),
        out_specs=(rows, rows, rows),
        check_vma=False,
    )
```

```python
import math

import jax
import jax.numpy as jnp
import numpy as np
from jax import lax
from jax.experimental import pallas as pl
from jax.experimental.pallas import tpu as pltpu
from jax.sharding import Mesh, PartitionSpec as P

AXES = ("z", "yh", "c", "x", "yl")
SIZES = (8, 2, 2, 4, 2)
PLANE = ("yh", "x", "yl")
ROWS = 128
WIDTH = 128
NDOCS = 16
TILE = 2048
RUN = 1024
PACK = 272
LOG2E = math.log2(math.e)
SCALE = 128.0 ** -0.5
SLOTS_COST = pl.CostEstimate(flops=7600000000, bytes_accessed=4 << 20, transcendentals=0)
SPREAD_COST = pl.CostEstimate(flops=10**9, bytes_accessed=2 << 20, transcendentals=0)
PAIR_COST = pl.CostEstimate(flops=9000000000, bytes_accessed=1 << 20, transcendentals=0)
BF = jnp.bfloat16
F32 = jnp.float32
ONE = jax.ShapeDtypeStruct((WIDTH, ROWS), BF)
TWO = jax.ShapeDtypeStruct((2, WIDTH, ROWS), BF)
KV = jax.ShapeDtypeStruct((16, 2 * ROWS, WIDTH), BF)


def pairs_along_z(k, both_ways, back):
    pairs = []
    for i in range(256):
        z, yh, c, x, yl = (int(v) for v in np.unravel_index(i, SIZES))
        t = z - k + 8 if both_ways and c == 1 else z + k
        if z < t < 8:
            j = int(np.ravel_multi_index((t, yh, c, x, yl), SIZES))
            pairs.append((j, i) if back else (i, j))
    return pairs


def call(body, out_shape, *args, smem=0, scratch=(), cost=None, out_specs=None):
    specs = [pl.BlockSpec(memory_space=pltpu.SMEM)] * smem
    specs += [pl.BlockSpec(memory_space=pltpu.VMEM)] * (len(args) - smem)
    return pl.pallas_call(
        body,
        out_shape=out_shape,
        in_specs=specs,
        **({} if out_specs is None else {"out_specs": out_specs}),
        scratch_shapes=scratch,
        cost_estimate=cost,
        compiler_params=pltpu.CompilerParams(vmem_limit_bytes=32 * 1024 * 1024),
    )(*args)


def split3(x):
    a = x.astype(BF)
    r = x - a.astype(F32)
    b = r.astype(BF)
    c = (r - b.astype(F32)).astype(BF)
    return a, b, c


def slot_of(s, z, c):
    k = s % 5 if s < 5 else s - 4
    if k in (0, 4):
        return z + k, c
    near = jnp.where(c == 0, z + k, z - k + 8)
    far = jnp.where(c == 0, z - k + 8, z + k)
    return (near, c) if s < 5 else (far, 1 - c)


def prep_kernel(
    q_hbm, g_hbm, o_hbm, lse_hbm, len_hbm, allow_hbm,
    pack_ref, at_ref,
    o_s, lse_s, len_s, allow_s, sems,
):
    loads = [
        pltpu.make_async_copy(g_hbm, pack_ref.at[128:256], sems.at[0]),
        pltpu.make_async_copy(o_hbm, o_s, sems.at[1]),
        pltpu.make_async_copy(lse_hbm, lse_s, sems.at[2]),
        pltpu.make_async_copy(len_hbm, len_s, sems.at[3]),
        pltpu.make_async_copy(allow_hbm, allow_s, sems.at[4]),
        pltpu.make_async_copy(q_hbm, pack_ref.at[0:128], sems.at[5]),
    ]
    for copy in loads:
        copy.start()
    for copy in loads[:3]:
        copy.wait()
    prod = pack_ref[128:256].astype(F32) * o_s[...].astype(F32)
    delta = jnp.sum(prod.T, axis=0, keepdims=True)
    lse2 = lse_s[...] * LOG2E
    parts = split3(lse2) + split3(delta)
    stats = [p.astype(F32) for p in parts] + [jnp.zeros((10, ROWS), F32)]
    pack_ref[256:272] = jnp.concatenate(stats, axis=0).astype(BF)

    loads[3].wait()
    loads[4].wait()
    z, yh, c = lax.axis_index("z"), lax.axis_index("yh"), lax.axis_index("c")
    off = (lax.axis_index("x") * 2 + lax.axis_index("yl")) * ROWS
    ends = []
    total = jnp.int32(0)
    for d in range(NDOCS):
        total = total + len_s[d]
        ends.append(total)
    lane = lax.broadcasted_iota(jnp.int32, (1, 2 * ROWS), 1)
    key_base = z * (2 * TILE) + c * RUN
    flag_lane = lax.broadcasted_iota(jnp.int32, (8, 2 * ROWS), 1)
    live = jnp.where(flag_lane == 16, key_base, 0)
    pos_all = []
    for s in range(8):
        zq, cq = slot_of(s, z, c)
        low = zq * (2 * TILE) + yh * TILE + off
        pos_all.append(
            jnp.where(lane < ROWS, low + cq * RUN + lane, low + (1 - cq) * RUN - ROWS + lane)
        )
        low_start = jnp.int32(0)
        for e in ends:
            low_start = jnp.where(e <= low, e, low_start)
        for t in range(2):
            b = key_base + t * TILE
            ok = allow_s[jnp.minimum(2 * zq + yh, 15), 2 * z + t] == 1
            ok = ok & (zq < 8) & (b <= low + RUN + ROWS - 1) & (b + RUN - 1 >= low_start)
            live = jnp.where(flag_lane == 8 * t + s, ok.astype(jnp.int32), live)
    pos = jnp.concatenate(pos_all, axis=0)
    start = jnp.zeros_like(pos)
    for e in ends:
        start = jnp.where(pos >= e, e, start)
    for s in range(8):
        at_ref[s, 0:1] = start[s : s + 1]
        at_ref[s, 1:2] = pos[s : s + 1]
    at_ref[8] = live
    loads[5].wait()


def prep(*args):
    hbm = pl.BlockSpec(memory_space=pl.ANY)
    vmem = pl.BlockSpec(memory_space=pltpu.VMEM)
    return pl.pallas_call(
        prep_kernel,
        out_shape=(
            jax.ShapeDtypeStruct((PACK, WIDTH), BF),
            jax.ShapeDtypeStruct((9, 8, 2 * ROWS), jnp.int32),
        ),
        in_specs=[hbm] * 6,
        out_specs=(vmem, vmem),
        scratch_shapes=[
            pltpu.VMEM((ROWS, WIDTH), BF),
            pltpu.VMEM((1, ROWS), F32),
            pltpu.SMEM((NDOCS,), jnp.int32),
            pltpu.SMEM((16, 16), jnp.int32),
            pltpu.SemaphoreType.DMA((6,)),
        ],
    )(*args)


def spread_kernel(k_hbm, v_hbm, kv_hbm, kv_s, sems):
    loads = [
        pltpu.make_async_copy(k_hbm, kv_s.at[0:128], sems.at[0]),
        pltpu.make_async_copy(v_hbm, kv_s.at[128:256], sems.at[1]),
    ]
    for copy in loads:
        copy.start()
    for copy in loads:
        copy.wait()
    stores = [pltpu.make_async_copy(kv_s, kv_hbm.at[n], sems.at[2 + n]) for n in range(16)]
    for copy in stores:
        copy.start()
    for copy in stores:
        copy.wait()


def spread(*args):
    hbm = pl.BlockSpec(memory_space=pl.ANY)
    return pl.pallas_call(
        spread_kernel,
        out_shape=KV,
        in_specs=[hbm] * 2,
        out_specs=hbm,
        scratch_shapes=[pltpu.VMEM((2 * ROWS, WIDTH), BF), pltpu.SemaphoreType.DMA((18,))],
        cost_estimate=SPREAD_COST,
    )(*args)


def stack_kernel(own_ref, other_ref, after, both_ref, sems):
    copies = [
        pltpu.make_async_copy(ref, both_ref.at[n], sems.at[n])
        for n, ref in enumerate((own_ref, other_ref))
    ]
    for copy in copies:
        copy.start()
    for copy in copies:
        copy.wait()


def stack(*args):
    hbm = pl.BlockSpec(memory_space=pl.ANY)
    return pl.pallas_call(
        stack_kernel,
        out_shape=jax.ShapeDtypeStruct((2, PACK, WIDTH), BF),
        in_specs=[hbm] * 3,
        out_specs=pl.BlockSpec(memory_space=pltpu.VMEM),
        scratch_shapes=[pltpu.SemaphoreType.DMA((2,))],
        compiler_params=pltpu.CompilerParams(vmem_limit_bytes=32 * 1024 * 1024),
    )(*args)


def slots_kernel(
    own_ref, own_x_ref, m1_ref, m2_ref, m3_ref, m4_ref, x1_ref, x2_ref, x3_ref, x4_ref,
    q_ref, g_ref, st_ref,
):
    slots = (
        ((own_ref, None), (own_x_ref, None)),
        ((m1_ref, 0), (m1_ref, 1)),
        ((m2_ref, 0), (m2_ref, 1)),
        ((m3_ref, 0), (m3_ref, 1)),
        ((m4_ref, None), (x4_ref, None)),
        ((x1_ref, 0), (x1_ref, 1)),
        ((x2_ref, 0), (x2_ref, 1)),
        ((x3_ref, 0), (x3_ref, 1)),
    )
    for s, halves in enumerate(slots):
        stats = []
        for half, (ref, i) in enumerate(halves):
            rows = slice(half * ROWS, (half + 1) * ROWS)
            q_ref[s, rows] = ref[0:128] if i is None else ref[i, 0:128]
            g_ref[s, rows] = ref[128:256] if i is None else ref[i, 128:256]
            stats.append((ref[256:272] if i is None else ref[i, 256:272]).astype(F32))
        st = jnp.concatenate(stats, axis=1)
        st_ref[s, 0:1] = st[0:1] + st[1:2] + st[2:3]
        st_ref[s, 1:2] = st[3:4] + st[4:5] + st[5:6]


def slots(*args):
    block = jax.ShapeDtypeStruct((8, 2 * ROWS, WIDTH), BF)
    stats = jax.ShapeDtypeStruct((8, 8, 2 * ROWS), F32)
    return call(slots_kernel, (block, block, stats), *args, cost=SLOTS_COST)


def grad_kernel(
    kv_ref, q_ref, g_ref, st_ref, at_ref,
    dkv_hbm, d0_ref, d1_ref, d2_ref, d3_ref, d4_ref, dx_ref,
    live_ref, kt_s, dk_acc, dv_acc, dqt_s, out_s, sems,
):
    flags = pltpu.make_async_copy(at_ref.at[8], live_ref, sems.at[2])
    flags.start()
    row = lax.broadcasted_iota(jnp.int32, (RUN, 1), 0)
    dqt_s[...] = jnp.zeros_like(dqt_s)
    stores = []
    for t in range(2):
        kt_s[...] = kv_ref[8 * t : 8 * t + 8, 0:128, :].reshape(RUN, WIDTH).T
        dk_acc[...] = jnp.zeros_like(dk_acc)
        dv_acc[...] = jnp.zeros_like(dv_acc)
        if t == 0:
            flags.wait()
        b = live_ref[0, 16] + t * TILE

        def slot_step(s, carry):
            @pl.when(live_ref[0, 8 * t + s] == 1)
            def _unit():
                q = q_ref[s]
                g = g_ref[s]
                lse2 = st_ref[s, 0:1]
                delta = st_ref[s, 1:2]
                start = at_ref[s, 0:1]
                pos = at_ref[s, 1:2]
                k = kv_ref[8 * t : 8 * t + 8, 0:128, :].reshape(RUN, WIDTH)
                v = kv_ref[8 * t : 8 * t + 8, 128:256, :].reshape(RUN, WIDTH)
                sc = lax.dot_general(k, q, (((1,), (1,)), ((), ())), preferred_element_type=F32)
                dp = lax.dot_general(v, g, (((1,), (1,)), ((), ())), preferred_element_type=F32)
                key = b + row
                vis = (key >= start) & (key <= pos)
                p = jnp.where(vis, jnp.exp2(sc * (SCALE * LOG2E) - lse2), 0.0)
                ds = (p * (dp - delta)).astype(BF)
                dv_acc[...] += jnp.dot(p.astype(BF), g, preferred_element_type=F32)
                dk_acc[...] += jnp.dot(ds, q, preferred_element_type=F32)
                dqt_s[s] += jnp.dot(kt_s[...], ds, preferred_element_type=F32)

            return carry

        lax.fori_loop(0, 8, slot_step, 0)
        for n in range(8):
            rows = slice(n * ROWS, (n + 1) * ROWS)
            out_s[8 * t + n, 0:128] = dk_acc[rows].astype(BF)
            out_s[8 * t + n, 128:256] = dv_acc[rows].astype(BF)
        part = pl.ds(8 * t, 8)
        stores.append(pltpu.make_async_copy(out_s.at[part], dkv_hbm.at[part], sems.at[t]))
        stores[t].start()

    def term(s, half):
        return dqt_s[s, :, half * ROWS : (half + 1) * ROWS].astype(BF)

    d0_ref[...] = term(0, 0)
    d4_ref[...] = term(4, 0)
    for k, out in enumerate((d1_ref, d2_ref, d3_ref)):
        for half in range(2):
            out[half] = term(k + 1, half)
            dx_ref[2 * k + half] = term(k + 5, half)
    dx_ref[6] = term(0, 1)
    dx_ref[7] = term(4, 1)
    for copy in stores:
        copy.wait()


def grads(*args):
    vmem = pl.BlockSpec(memory_space=pltpu.VMEM)
    return call(
        grad_kernel,
        (KV, ONE, TWO, TWO, TWO, ONE, jax.ShapeDtypeStruct((8, WIDTH, ROWS), BF)),
        *args,
        out_specs=(pl.BlockSpec(memory_space=pl.ANY),) + (vmem,) * 6,
        scratch=[
            pltpu.SMEM((8, 2 * ROWS), jnp.int32),
            pltpu.VMEM((WIDTH, RUN), BF),
            pltpu.VMEM((RUN, WIDTH), F32),
            pltpu.VMEM((RUN, WIDTH), F32),
            pltpu.VMEM((8, WIDTH, 2 * ROWS), F32),
            pltpu.VMEM((16, 2 * ROWS, WIDTH), BF),
            pltpu.SemaphoreType.DMA((3,)),
        ],
    )


def pair_kernel(d0, d1, d2, d3, d4, got, s0, s1, s2, s3, s4):
    for k, (a, out) in enumerate(((d1, s1), (d2, s2), (d3, s3))):
        out[...] = (a[...].astype(F32) + got[2 * k : 2 * k + 2].astype(F32)).astype(BF)
    s0[...] = (d0[...].astype(F32) + got[6].astype(F32)).astype(BF)
    s4[...] = (d4[...].astype(F32) + got[7].astype(F32)).astype(BF)


def column_kernel(s0, e1, e2, e3, e4, keep, send):
    total = e1[...].astype(F32) + e2[...].astype(F32) + e3[...].astype(F32)
    keep[...] = total[0] + e4[...].astype(F32) + s0[...].astype(F32)
    send[...] = total[1].astype(BF)


def last_kernel(dkv_all, keep, got, dq_ref, dk_ref, dv_ref):
    dkv = dkv_all[0].astype(F32)
    for n in range(1, 16):
        dkv = dkv + dkv_all[n].astype(F32)
    dk_ref[...] = (dkv[:ROWS] * SCALE).astype(BF)
    dv_ref[...] = dkv[ROWS:].astype(BF)
    dq_ref[...] = ((keep[...] + got[...].astype(F32)).T * SCALE).astype(BF)


def on_device(
    queries, key_rows, value_rows, outputs, out_grad, log_sums, doc_lengths, tile_allowed
):
    def swap(x):
        return lax.ppermute(x, "c", [(0, 1), (1, 0)])

    def along_z(x, k, both_ways=True, back=False):
        return lax.ppermute(x, AXES, pairs_along_z(k, both_ways, back))

    own, at = prep(
        queries, out_grad, outputs, log_sums.reshape(1, ROWS), doc_lengths, tile_allowed
    )
    own_x = swap(own)
    kv_out = spread(key_rows, value_rows)
    kv = lax.all_to_all(kv_out, PLANE, 0, 0, tiled=True)
    both = stack(own, own_x, kv_out)
    mine = [along_z(both, k, back=True) for k in (1, 2, 3)]
    mine.append(along_z(own, 4, both_ways=False, back=True))
    theirs = [swap(m) for m in mine]

    q, g, stats = slots(own, own_x, *mine, *theirs)
    dkv, d0, d1, d2, d3, d4, dx = grads(kv, q, g, stats, at)
    dkv_all = lax.all_to_all(dkv, PLANE, 0, 0, tiled=True)
    s0, s1, s2, s3, s4 = call(
        pair_kernel, (ONE, TWO, TWO, TWO, ONE), d0, d1, d2, d3, d4, swap(dx), cost=PAIR_COST
    )
    e1, e2, e3 = (along_z(s, k) for k, s in ((1, s1), (2, s2), (3, s3)))
    e4 = along_z(s4, 4, both_ways=False)
    keep, send = call(
        column_kernel,
        (jax.ShapeDtypeStruct((WIDTH, ROWS), F32), ONE),
        s0, e1, e2, e3, e4,
    )
    out = jax.ShapeDtypeStruct((ROWS, WIDTH), BF)
    return call(last_kernel, (out, out, out), dkv_all, keep, swap(send))


def solution(mesh):
    fine = Mesh(mesh.devices.reshape(SIZES), AXES)
    rows, vec = P(AXES, None), P(AXES)
    return jax.shard_map(
        on_device,
        mesh=fine,
        in_specs=(rows, rows, rows, rows, rows, vec, P(), P()),
        out_specs=(rows, rows, rows),
        check_vma=False,
    )
```

```python
import math

import jax
import jax.numpy as jnp
import numpy as np
from jax import lax
from jax.experimental import pallas as pl
from jax.experimental.pallas import tpu as pltpu
from jax.sharding import Mesh, PartitionSpec as P

AXES = ("z", "yh", "c", "x", "yl")
SIZES = (8, 2, 2, 4, 2)
PLANE = ("yh", "x", "yl")
ROWS = 128
WIDTH = 128
NDOCS = 16
TILE = 2048
RUN = 1024
PACK = 272
LOG2E = math.log2(math.e)
SCALE = 128.0 ** -0.5
SLOTS_COST = pl.CostEstimate(flops=7600000000, bytes_accessed=4 << 20, transcendentals=0)
SPREAD_COST = pl.CostEstimate(flops=10**9, bytes_accessed=2 << 20, transcendentals=0)
PAIR_COST = pl.CostEstimate(flops=9000000000, bytes_accessed=1 << 20, transcendentals=0)
BF = jnp.bfloat16
F32 = jnp.float32
ONE = jax.ShapeDtypeStruct((WIDTH, ROWS), BF)
TWO = jax.ShapeDtypeStruct((2, WIDTH, ROWS), BF)
KV = jax.ShapeDtypeStruct((16, 2 * ROWS, WIDTH), BF)


def pairs_along_z(k, both_ways, back):
    pairs = []
    for i in range(256):
        z, yh, c, x, yl = (int(v) for v in np.unravel_index(i, SIZES))
        t = z - k + 8 if both_ways and c == 1 else z + k
        if z < t < 8:
            j = int(np.ravel_multi_index((t, yh, c, x, yl), SIZES))
            pairs.append((j, i) if back else (i, j))
    return pairs


def call(body, out_shape, *args, smem=0, scratch=(), cost=None, out_specs=None):
    specs = [pl.BlockSpec(memory_space=pltpu.SMEM)] * smem
    specs += [pl.BlockSpec(memory_space=pltpu.VMEM)] * (len(args) - smem)
    return pl.pallas_call(
        body,
        out_shape=out_shape,
        in_specs=specs,
        **({} if out_specs is None else {"out_specs": out_specs}),
        scratch_shapes=scratch,
        cost_estimate=cost,
        compiler_params=pltpu.CompilerParams(vmem_limit_bytes=32 * 1024 * 1024),
    )(*args)


def split3(x):
    a = x.astype(BF)
    r = x - a.astype(F32)
    b = r.astype(BF)
    c = (r - b.astype(F32)).astype(BF)
    return a, b, c


def slot_of(s, z, c):
    k = s % 5 if s < 5 else s - 4
    if k in (0, 4):
        return z + k, c
    near = jnp.where(c == 0, z + k, z - k + 8)
    far = jnp.where(c == 0, z - k + 8, z + k)
    return (near, c) if s < 5 else (far, 1 - c)


def prep_kernel(
    q_hbm, g_hbm, o_hbm, lse_hbm, pack_ref, o_s, lse_s, sems
):
    loads = [
        pltpu.make_async_copy(g_hbm, pack_ref.at[128:256], sems.at[0]),
        pltpu.make_async_copy(o_hbm, o_s, sems.at[1]),
        pltpu.make_async_copy(lse_hbm, lse_s, sems.at[2]),
        pltpu.make_async_copy(q_hbm, pack_ref.at[0:128], sems.at[3]),
    ]
    for copy in loads:
        copy.start()
    for copy in loads[:3]:
        copy.wait()
    prod = pack_ref[128:256].astype(F32) * o_s[...].astype(F32)
    delta = jnp.sum(prod.T, axis=0, keepdims=True)
    lse2 = lse_s[...] * LOG2E
    parts = split3(lse2) + split3(delta)
    stats = [p.astype(F32) for p in parts] + [jnp.zeros((10, ROWS), F32)]
    pack_ref[256:272] = jnp.concatenate(stats, axis=0).astype(BF)

    loads[3].wait()


def prep(*args):
    return pl.pallas_call(
        prep_kernel,
        out_shape=jax.ShapeDtypeStruct((PACK, WIDTH), BF),
        in_specs=[pl.BlockSpec(memory_space=pl.ANY)] * 4,
        out_specs=pl.BlockSpec(memory_space=pltpu.VMEM),
        scratch_shapes=[
            pltpu.VMEM((ROWS, WIDTH), BF),
            pltpu.VMEM((1, ROWS), F32),
            pltpu.SemaphoreType.DMA((4,)),
        ],
    )(*args)


def plan_kernel(len_hbm, allow_hbm, after, at_ref, len_s, allow_s, sems):
    loads = [
        pltpu.make_async_copy(len_hbm, len_s, sems.at[0]),
        pltpu.make_async_copy(allow_hbm, allow_s, sems.at[1]),
    ]
    for copy in loads:
        copy.start()
    for copy in loads:
        copy.wait()
    z, yh, c = lax.axis_index("z"), lax.axis_index("yh"), lax.axis_index("c")
    off = (lax.axis_index("x") * 2 + lax.axis_index("yl")) * ROWS
    ends = []
    total = jnp.int32(0)
    for d in range(NDOCS):
        total = total + len_s[d]
        ends.append(total)
    lane = lax.broadcasted_iota(jnp.int32, (1, 2 * ROWS), 1)
    key_base = z * (2 * TILE) + c * RUN
    flag_lane = lax.broadcasted_iota(jnp.int32, (8, 2 * ROWS), 1)
    live = jnp.where(flag_lane == 16, key_base, 0)
    pos_all = []
    for s in range(8):
        zq, cq = slot_of(s, z, c)
        low = zq * (2 * TILE) + yh * TILE + off
        pos_all.append(
            jnp.where(lane < ROWS, low + cq * RUN + lane, low + (1 - cq) * RUN - ROWS + lane)
        )
        low_start = jnp.int32(0)
        for e in ends:
            low_start = jnp.where(e <= low, e, low_start)
        for t in range(2):
            b = key_base + t * TILE
            ok = allow_s[jnp.minimum(2 * zq + yh, 15), 2 * z + t] == 1
            ok = ok & (zq < 8) & (b <= low + RUN + ROWS - 1) & (b + RUN - 1 >= low_start)
            live = jnp.where(flag_lane == 8 * t + s, ok.astype(jnp.int32), live)
    pos = jnp.concatenate(pos_all, axis=0)
    start = jnp.zeros_like(pos)
    for e in ends:
        start = jnp.where(pos >= e, e, start)
    for s in range(8):
        at_ref[s, 0:1] = start[s : s + 1]
        at_ref[s, 1:2] = pos[s : s + 1]
    at_ref[8] = live


def plan(*args):
    return pl.pallas_call(
        plan_kernel,
        out_shape=jax.ShapeDtypeStruct((9, 8, 2 * ROWS), jnp.int32),
        in_specs=[pl.BlockSpec(memory_space=pl.ANY)] * 3,
        out_specs=pl.BlockSpec(memory_space=pltpu.VMEM),
        scratch_shapes=[
            pltpu.SMEM((NDOCS,), jnp.int32),
            pltpu.SMEM((16, 16), jnp.int32),
            pltpu.SemaphoreType.DMA((2,)),
        ],
        cost_estimate=SPREAD_COST,
        compiler_params=pltpu.CompilerParams(vmem_limit_bytes=32 * 1024 * 1024),
    )(*args)


def spread_kernel(k_hbm, v_hbm, kv_hbm, kv_s, sems):
    loads = [
        pltpu.make_async_copy(k_hbm, kv_s.at[0:128], sems.at[0]),
        pltpu.make_async_copy(v_hbm, kv_s.at[128:256], sems.at[1]),
    ]
    for copy in loads:
        copy.start()
    for copy in loads:
        copy.wait()
    stores = [pltpu.make_async_copy(kv_s, kv_hbm.at[n], sems.at[2 + n]) for n in range(16)]
    for copy in stores:
        copy.start()
    for copy in stores:
        copy.wait()


def spread(*args):
    hbm = pl.BlockSpec(memory_space=pl.ANY)
    return pl.pallas_call(
        spread_kernel,
        out_shape=KV,
        in_specs=[hbm] * 2,
        out_specs=hbm,
        scratch_shapes=[pltpu.VMEM((2 * ROWS, WIDTH), BF), pltpu.SemaphoreType.DMA((18,))],
        cost_estimate=SPREAD_COST,
    )(*args)


def stack_kernel(own_ref, other_ref, after, both_ref, sems):
    copies = [
        pltpu.make_async_copy(ref, both_ref.at[n], sems.at[n])
        for n, ref in enumerate((own_ref, other_ref))
    ]
    for copy in copies:
        copy.start()
    for copy in copies:
        copy.wait()


def stack(*args):
    hbm = pl.BlockSpec(memory_space=pl.ANY)
    return pl.pallas_call(
        stack_kernel,
        out_shape=jax.ShapeDtypeStruct((2, PACK, WIDTH), BF),
        in_specs=[hbm] * 3,
        out_specs=pl.BlockSpec(memory_space=pltpu.VMEM),
        scratch_shapes=[pltpu.SemaphoreType.DMA((2,))],
        compiler_params=pltpu.CompilerParams(vmem_limit_bytes=32 * 1024 * 1024),
    )(*args)


def slots_kernel(
    own_ref, own_x_ref, m1_ref, m2_ref, m3_ref, m4_ref, x1_ref, x2_ref, x3_ref, x4_ref,
    q_ref, g_ref, st_ref,
):
    slots = (
        ((own_ref, None), (own_x_ref, None)),
        ((m1_ref, 0), (m1_ref, 1)),
        ((m2_ref, 0), (m2_ref, 1)),
        ((m3_ref, 0), (m3_ref, 1)),
        ((m4_ref, None), (x4_ref, None)),
        ((x1_ref, 0), (x1_ref, 1)),
        ((x2_ref, 0), (x2_ref, 1)),
        ((x3_ref, 0), (x3_ref, 1)),
    )
    for s, halves in enumerate(slots):
        stats = []
        for half, (ref, i) in enumerate(halves):
            rows = slice(half * ROWS, (half + 1) * ROWS)
            q_ref[s, rows] = ref[0:128] if i is None else ref[i, 0:128]
            g_ref[s, rows] = ref[128:256] if i is None else ref[i, 128:256]
            stats.append((ref[256:272] if i is None else ref[i, 256:272]).astype(F32))
        st = jnp.concatenate(stats, axis=1)
        st_ref[s, 0:1] = st[0:1] + st[1:2] + st[2:3]
        st_ref[s, 1:2] = st[3:4] + st[4:5] + st[5:6]


def slots(*args):
    block = jax.ShapeDtypeStruct((8, 2 * ROWS, WIDTH), BF)
    stats = jax.ShapeDtypeStruct((8, 8, 2 * ROWS), F32)
    return call(slots_kernel, (block, block, stats), *args, cost=SLOTS_COST)


def grad_kernel(
    kv_ref, q_ref, g_ref, st_ref, at_ref,
    dkv_hbm, d0_ref, d1_ref, d2_ref, d3_ref, d4_ref, dx_ref,
    live_ref, kt_s, dk_acc, dv_acc, dqt_s, out_s, sems,
):
    flags = pltpu.make_async_copy(at_ref.at[8], live_ref, sems.at[2])
    flags.start()
    row = lax.broadcasted_iota(jnp.int32, (RUN, 1), 0)
    dqt_s[...] = jnp.zeros_like(dqt_s)
    stores = []
    for t in range(2):
        kt_s[...] = kv_ref[8 * t : 8 * t + 8, 0:128, :].reshape(RUN, WIDTH).T
        dk_acc[...] = jnp.zeros_like(dk_acc)
        dv_acc[...] = jnp.zeros_like(dv_acc)
        if t == 0:
            flags.wait()
        b = live_ref[0, 16] + t * TILE

        def slot_step(s, carry):
            @pl.when(live_ref[0, 8 * t + s] == 1)
            def _unit():
                q = q_ref[s]
                g = g_ref[s]
                lse2 = st_ref[s, 0:1]
                delta = st_ref[s, 1:2]
                start = at_ref[s, 0:1]
                pos = at_ref[s, 1:2]
                k = kv_ref[8 * t : 8 * t + 8, 0:128, :].reshape(RUN, WIDTH)
                v = kv_ref[8 * t : 8 * t + 8, 128:256, :].reshape(RUN, WIDTH)
                sc = lax.dot_general(k, q, (((1,), (1,)), ((), ())), preferred_element_type=F32)
                dp = lax.dot_general(v, g, (((1,), (1,)), ((), ())), preferred_element_type=F32)
                key = b + row
                vis = (key >= start) & (key <= pos)
                p = jnp.where(vis, jnp.exp2(sc * (SCALE * LOG2E) - lse2), 0.0)
                ds = (p * (dp - delta)).astype(BF)
                dv_acc[...] += jnp.dot(p.astype(BF), g, preferred_element_type=F32)
                dk_acc[...] += jnp.dot(ds, q, preferred_element_type=F32)
                dqt_s[s] += jnp.dot(kt_s[...], ds, preferred_element_type=F32)

            return carry

        lax.fori_loop(0, 8, slot_step, 0)
        for n in range(8):
            rows = slice(n * ROWS, (n + 1) * ROWS)
            out_s[8 * t + n, 0:128] = dk_acc[rows].astype(BF)
            out_s[8 * t + n, 128:256] = dv_acc[rows].astype(BF)
        part = pl.ds(8 * t, 8)
        stores.append(pltpu.make_async_copy(out_s.at[part], dkv_hbm.at[part], sems.at[t]))
        stores[t].start()

    def term(s, half):
        return dqt_s[s, :, half * ROWS : (half + 1) * ROWS].astype(BF)

    d0_ref[...] = term(0, 0)
    d4_ref[...] = term(4, 0)
    for k, out in enumerate((d1_ref, d2_ref, d3_ref)):
        for half in range(2):
            out[half] = term(k + 1, half)
            dx_ref[2 * k + half] = term(k + 5, half)
    dx_ref[6] = term(0, 1)
    dx_ref[7] = term(4, 1)
    for copy in stores:
        copy.wait()


def grads(*args):
    vmem = pl.BlockSpec(memory_space=pltpu.VMEM)
    return call(
        grad_kernel,
        (KV, ONE, TWO, TWO, TWO, ONE, jax.ShapeDtypeStruct((8, WIDTH, ROWS), BF)),
        *args,
        out_specs=(pl.BlockSpec(memory_space=pl.ANY),) + (vmem,) * 6,
        scratch=[
            pltpu.SMEM((8, 2 * ROWS), jnp.int32),
            pltpu.VMEM((WIDTH, RUN), BF),
            pltpu.VMEM((RUN, WIDTH), F32),
            pltpu.VMEM((RUN, WIDTH), F32),
            pltpu.VMEM((8, WIDTH, 2 * ROWS), F32),
            pltpu.VMEM((16, 2 * ROWS, WIDTH), BF),
            pltpu.SemaphoreType.DMA((3,)),
        ],
    )


def pair_kernel(d0, d1, d2, d3, d4, got, s0, s1, s2, s3, s4):
    for k, (a, out) in enumerate(((d1, s1), (d2, s2), (d3, s3))):
        out[...] = (a[...].astype(F32) + got[2 * k : 2 * k + 2].astype(F32)).astype(BF)
    s0[...] = (d0[...].astype(F32) + got[6].astype(F32)).astype(BF)
    s4[...] = (d4[...].astype(F32) + got[7].astype(F32)).astype(BF)


def column_kernel(s0, e1, e2, e3, e4, keep, send):
    total = e1[...].astype(F32) + e2[...].astype(F32) + e3[...].astype(F32)
    keep[...] = total[0] + e4[...].astype(F32) + s0[...].astype(F32)
    send[...] = total[1].astype(BF)


def last_kernel(dkv_all, keep, got, dq_ref, dk_ref, dv_ref):
    dkv = dkv_all[0].astype(F32)
    for n in range(1, 16):
        dkv = dkv + dkv_all[n].astype(F32)
    dk_ref[...] = (dkv[:ROWS] * SCALE).astype(BF)
    dv_ref[...] = dkv[ROWS:].astype(BF)
    dq_ref[...] = ((keep[...] + got[...].astype(F32)).T * SCALE).astype(BF)


def on_device(
    queries, key_rows, value_rows, outputs, out_grad, log_sums, doc_lengths, tile_allowed
):
    def swap(x):
        return lax.ppermute(x, "c", [(0, 1), (1, 0)])

    def along_z(x, k, both_ways=True, back=False):
        return lax.ppermute(x, AXES, pairs_along_z(k, both_ways, back))

    own = prep(queries, out_grad, outputs, log_sums.reshape(1, ROWS))
    own_x = swap(own)
    kv_out = spread(key_rows, value_rows)
    kv = lax.all_to_all(kv_out, PLANE, 0, 0, tiled=True)
    both = stack(own, own_x, kv_out)
    mine = [along_z(both, k, back=True) for k in (1, 2, 3)]
    mine.append(along_z(own, 4, both_ways=False, back=True))
    at = plan(doc_lengths, tile_allowed, mine[0])
    theirs = [swap(m) for m in mine]

    q, g, stats = slots(own, own_x, *mine, *theirs)
    dkv, d0, d1, d2, d3, d4, dx = grads(kv, q, g, stats, at)
    dkv_all = lax.all_to_all(dkv, PLANE, 0, 0, tiled=True)
    s0, s1, s2, s3, s4 = call(
        pair_kernel, (ONE, TWO, TWO, TWO, ONE), d0, d1, d2, d3, d4, swap(dx), cost=PAIR_COST
    )
    e1, e2, e3 = (along_z(s, k) for k, s in ((1, s1), (2, s2), (3, s3)))
    e4 = along_z(s4, 4, both_ways=False)
    keep, send = call(
        column_kernel,
        (jax.ShapeDtypeStruct((WIDTH, ROWS), F32), ONE),
        s0, e1, e2, e3, e4,
    )
    out = jax.ShapeDtypeStruct((ROWS, WIDTH), BF)
    return call(last_kernel, (out, out, out), dkv_all, keep, swap(send))


def solution(mesh):
    fine = Mesh(mesh.devices.reshape(SIZES), AXES)
    rows, vec = P(AXES, None), P(AXES)
    return jax.shard_map(
        on_device,
        mesh=fine,
        in_specs=(rows, rows, rows, rows, rows, vec, P(), P()),
        out_specs=(rows, rows, rows),
        check_vma=False,
    )
```

```python
import math

import jax
import jax.numpy as jnp
import numpy as np
from jax import lax
from jax.experimental import pallas as pl
from jax.experimental.pallas import tpu as pltpu
from jax.sharding import Mesh, PartitionSpec as P

AXES = ("z", "yh", "c", "x", "yl")
SIZES = (8, 2, 2, 4, 2)
PLANE = ("yh", "x", "yl")
ROWS = 128
WIDTH = 128
NDOCS = 16
TILE = 2048
RUN = 1024
PACK = 272
LOG2E = math.log2(math.e)
SCALE = 128.0 ** -0.5
SLOTS_COST = pl.CostEstimate(flops=7600000000, bytes_accessed=4 << 20, transcendentals=0)
SPREAD_COST = pl.CostEstimate(flops=10**9, bytes_accessed=2 << 20, transcendentals=0)
PAIR_COST = pl.CostEstimate(flops=9000000000, bytes_accessed=1 << 20, transcendentals=0)
BF = jnp.bfloat16
F32 = jnp.float32
ONE = jax.ShapeDtypeStruct((WIDTH, ROWS), BF)
TWO = jax.ShapeDtypeStruct((2, WIDTH, ROWS), BF)
KV = jax.ShapeDtypeStruct((16, 2 * ROWS, WIDTH), BF)


def pairs_along_z(k, both_ways, back):
    pairs = []
    for i in range(256):
        z, yh, c, x, yl = (int(v) for v in np.unravel_index(i, SIZES))
        t = z - k + 8 if both_ways and c == 1 else z + k
        if z < t < 8:
            j = int(np.ravel_multi_index((t, yh, c, x, yl), SIZES))
            pairs.append((j, i) if back else (i, j))
    return pairs


def call(body, out_shape, *args, smem=0, scratch=(), cost=None, out_specs=None):
    specs = [pl.BlockSpec(memory_space=pltpu.SMEM)] * smem
    specs += [pl.BlockSpec(memory_space=pltpu.VMEM)] * (len(args) - smem)
    return pl.pallas_call(
        body,
        out_shape=out_shape,
        in_specs=specs,
        **({} if out_specs is None else {"out_specs": out_specs}),
        scratch_shapes=scratch,
        cost_estimate=cost,
        compiler_params=pltpu.CompilerParams(vmem_limit_bytes=32 * 1024 * 1024),
    )(*args)


def split3(x):
    a = x.astype(BF)
    r = x - a.astype(F32)
    b = r.astype(BF)
    c = (r - b.astype(F32)).astype(BF)
    return a, b, c


def slot_of(s, z, c):
    k = s % 5 if s < 5 else s - 4
    if k in (0, 4):
        return z + k, c
    near = jnp.where(c == 0, z + k, z - k + 8)
    far = jnp.where(c == 0, z - k + 8, z + k)
    return (near, c) if s < 5 else (far, 1 - c)


def prep_kernel(
    q_hbm, g_hbm, o_hbm, lse_hbm, pack_ref, o_s, lse_s, sems
):
    loads = [
        pltpu.make_async_copy(g_hbm, pack_ref.at[128:256], sems.at[0]),
        pltpu.make_async_copy(o_hbm, o_s, sems.at[1]),
        pltpu.make_async_copy(lse_hbm, lse_s, sems.at[2]),
        pltpu.make_async_copy(q_hbm, pack_ref.at[0:128], sems.at[3]),
    ]
    for copy in loads:
        copy.start()
    for copy in loads[:3]:
        copy.wait()
    prod = pack_ref[128:256].astype(F32) * o_s[...].astype(F32)
    delta = jnp.sum(prod.T, axis=0, keepdims=True)
    lse2 = lse_s[...] * LOG2E
    parts = split3(lse2) + split3(delta)
    stats = [p.astype(F32) for p in parts] + [jnp.zeros((10, ROWS), F32)]
    pack_ref[256:272] = jnp.concatenate(stats, axis=0).astype(BF)

    loads[3].wait()


def prep(*args):
    return pl.pallas_call(
        prep_kernel,
        out_shape=jax.ShapeDtypeStruct((PACK, WIDTH), BF),
        in_specs=[pl.BlockSpec(memory_space=pl.ANY)] * 4,
        out_specs=pl.BlockSpec(memory_space=pltpu.VMEM),
        scratch_shapes=[
            pltpu.VMEM((ROWS, WIDTH), BF),
            pltpu.VMEM((1, ROWS), F32),
            pltpu.SemaphoreType.DMA((4,)),
        ],
    )(*args)


def plan_kernel(len_hbm, allow_hbm, after, at_ref, len_s, allow_s, sems):
    loads = [
        pltpu.make_async_copy(len_hbm, len_s, sems.at[0]),
        pltpu.make_async_copy(allow_hbm, allow_s, sems.at[1]),
    ]
    for copy in loads:
        copy.start()
    for copy in loads:
        copy.wait()
    z, yh, c = lax.axis_index("z"), lax.axis_index("yh"), lax.axis_index("c")
    off = (lax.axis_index("x") * 2 + lax.axis_index("yl")) * ROWS
    ends = []
    total = jnp.int32(0)
    for d in range(NDOCS):
        total = total + len_s[d]
        ends.append(total)
    lane = lax.broadcasted_iota(jnp.int32, (1, 2 * ROWS), 1)
    key_base = z * (2 * TILE) + c * RUN
    flag_lane = lax.broadcasted_iota(jnp.int32, (8, 2 * ROWS), 1)
    live = jnp.where(flag_lane == 16, key_base, 0)
    pos_all = []
    for s in range(8):
        zq, cq = slot_of(s, z, c)
        low = zq * (2 * TILE) + yh * TILE + off
        pos_all.append(
            jnp.where(lane < ROWS, low + cq * RUN + lane, low + (1 - cq) * RUN - ROWS + lane)
        )
        low_start = jnp.int32(0)
        for e in ends:
            low_start = jnp.where(e <= low, e, low_start)
        for t in range(2):
            b = key_base + t * TILE
            ok = allow_s[jnp.minimum(2 * zq + yh, 15), 2 * z + t] == 1
            ok = ok & (zq < 8) & (b <= low + RUN + ROWS - 1) & (b + RUN - 1 >= low_start)
            live = jnp.where(flag_lane == 8 * t + s, ok.astype(jnp.int32), live)
    pos = jnp.concatenate(pos_all, axis=0)
    start = jnp.zeros_like(pos)
    for e in ends:
        start = jnp.where(pos >= e, e, start)
    for s in range(8):
        at_ref[s, 0:1] = start[s : s + 1]
        at_ref[s, 1:2] = pos[s : s + 1]
    at_ref[8] = live


def plan(*args):
    return pl.pallas_call(
        plan_kernel,
        out_shape=jax.ShapeDtypeStruct((9, 8, 2 * ROWS), jnp.int32),
        in_specs=[pl.BlockSpec(memory_space=pl.ANY)] * 3,
        out_specs=pl.BlockSpec(memory_space=pltpu.VMEM),
        scratch_shapes=[
            pltpu.SMEM((NDOCS,), jnp.int32),
            pltpu.SMEM((16, 16), jnp.int32),
            pltpu.SemaphoreType.DMA((2,)),
        ],
        cost_estimate=SPREAD_COST,
        compiler_params=pltpu.CompilerParams(vmem_limit_bytes=32 * 1024 * 1024),
    )(*args)


def spread_kernel(k_hbm, v_hbm, kv_hbm, kv_s, sems):
    loads = [
        pltpu.make_async_copy(k_hbm, kv_s.at[0:128], sems.at[0]),
        pltpu.make_async_copy(v_hbm, kv_s.at[128:256], sems.at[1]),
    ]
    for copy in loads:
        copy.start()
    for copy in loads:
        copy.wait()
    stores = [pltpu.make_async_copy(kv_s, kv_hbm.at[n], sems.at[2 + n]) for n in range(16)]
    for copy in stores:
        copy.start()
    for copy in stores:
        copy.wait()


def spread(*args):
    hbm = pl.BlockSpec(memory_space=pl.ANY)
    return pl.pallas_call(
        spread_kernel,
        out_shape=KV,
        in_specs=[hbm] * 2,
        out_specs=hbm,
        scratch_shapes=[pltpu.VMEM((2 * ROWS, WIDTH), BF), pltpu.SemaphoreType.DMA((18,))],
        cost_estimate=SPREAD_COST,
    )(*args)


def stack_kernel(own_ref, other_ref, after, both_ref, sems):
    copies = [
        pltpu.make_async_copy(ref, both_ref.at[n], sems.at[n])
        for n, ref in enumerate((own_ref, other_ref))
    ]
    for copy in copies:
        copy.start()
    for copy in copies:
        copy.wait()


def stack(*args):
    hbm = pl.BlockSpec(memory_space=pl.ANY)
    return pl.pallas_call(
        stack_kernel,
        out_shape=jax.ShapeDtypeStruct((2, PACK, WIDTH), BF),
        in_specs=[hbm] * 3,
        out_specs=pl.BlockSpec(memory_space=pltpu.VMEM),
        scratch_shapes=[pltpu.SemaphoreType.DMA((2,))],
        compiler_params=pltpu.CompilerParams(vmem_limit_bytes=32 * 1024 * 1024),
    )(*args)


def slots_kernel(
    own_ref, own_x_ref, m4_ref, m3_ref, m2_ref, m1_ref, x4_ref, x3_ref, x2_ref, x1_ref,
    q_ref, g_ref, st_ref,
):
    slots = (
        ((own_ref, None), (own_x_ref, None)),
        ((m1_ref, 0), (m1_ref, 1)),
        ((m2_ref, 0), (m2_ref, 1)),
        ((m3_ref, 0), (m3_ref, 1)),
        ((m4_ref, None), (x4_ref, None)),
        ((x1_ref, 0), (x1_ref, 1)),
        ((x2_ref, 0), (x2_ref, 1)),
        ((x3_ref, 0), (x3_ref, 1)),
    )
    for s, halves in enumerate(slots):
        stats = []
        for half, (ref, i) in enumerate(halves):
            rows = slice(half * ROWS, (half + 1) * ROWS)
            q_ref[s, rows] = ref[0:128] if i is None else ref[i, 0:128]
            g_ref[s, rows] = ref[128:256] if i is None else ref[i, 128:256]
            stats.append((ref[256:272] if i is None else ref[i, 256:272]).astype(F32))
        st = jnp.concatenate(stats, axis=1)
        st_ref[s, 0:1] = st[0:1] + st[1:2] + st[2:3]
        st_ref[s, 1:2] = st[3:4] + st[4:5] + st[5:6]


def slots(*args):
    block = jax.ShapeDtypeStruct((8, 2 * ROWS, WIDTH), BF)
    stats = jax.ShapeDtypeStruct((8, 8, 2 * ROWS), F32)
    return call(slots_kernel, (block, block, stats), *args, cost=SLOTS_COST)


def grad_kernel(
    kv_ref, q_ref, g_ref, st_ref, at_ref,
    dkv_hbm, d0_ref, d1_ref, d2_ref, d3_ref, d4_ref, dx_ref,
    live_ref, kt_s, dk_acc, dv_acc, dqt_s, out_s, sems,
):
    flags = pltpu.make_async_copy(at_ref.at[8], live_ref, sems.at[2])
    flags.start()
    row = lax.broadcasted_iota(jnp.int32, (RUN, 1), 0)
    dqt_s[...] = jnp.zeros_like(dqt_s)
    stores = []
    for t in range(2):
        kt_s[...] = kv_ref[8 * t : 8 * t + 8, 0:128, :].reshape(RUN, WIDTH).T
        dk_acc[...] = jnp.zeros_like(dk_acc)
        dv_acc[...] = jnp.zeros_like(dv_acc)
        if t == 0:
            flags.wait()
        b = live_ref[0, 16] + t * TILE

        def slot_step(s, carry):
            @pl.when(live_ref[0, 8 * t + s] == 1)
            def _unit():
                q = q_ref[s]
                g = g_ref[s]
                lse2 = st_ref[s, 0:1]
                delta = st_ref[s, 1:2]
                start = at_ref[s, 0:1]
                pos = at_ref[s, 1:2]
                k = kv_ref[8 * t : 8 * t + 8, 0:128, :].reshape(RUN, WIDTH)
                v = kv_ref[8 * t : 8 * t + 8, 128:256, :].reshape(RUN, WIDTH)
                sc = lax.dot_general(k, q, (((1,), (1,)), ((), ())), preferred_element_type=F32)
                dp = lax.dot_general(v, g, (((1,), (1,)), ((), ())), preferred_element_type=F32)
                key = b + row
                vis = (key >= start) & (key <= pos)
                p = jnp.where(vis, jnp.exp2(sc * (SCALE * LOG2E) - lse2), 0.0)
                ds = (p * (dp - delta)).astype(BF)
                dv_acc[...] += jnp.dot(p.astype(BF), g, preferred_element_type=F32)
                dk_acc[...] += jnp.dot(ds, q, preferred_element_type=F32)
                dqt_s[s] += jnp.dot(kt_s[...], ds, preferred_element_type=F32)

            return carry

        lax.fori_loop(0, 8, slot_step, 0)
        for n in range(8):
            rows = slice(n * ROWS, (n + 1) * ROWS)
            out_s[8 * t + n, 0:128] = dk_acc[rows].astype(BF)
            out_s[8 * t + n, 128:256] = dv_acc[rows].astype(BF)
        part = pl.ds(8 * t, 8)
        stores.append(pltpu.make_async_copy(out_s.at[part], dkv_hbm.at[part], sems.at[t]))
        stores[t].start()

    def term(s, half):
        return dqt_s[s, :, half * ROWS : (half + 1) * ROWS].astype(BF)

    d0_ref[...] = term(0, 0)
    d4_ref[...] = term(4, 0)
    for k, out in enumerate((d1_ref, d2_ref, d3_ref)):
        for half in range(2):
            out[half] = term(k + 1, half)
            dx_ref[2 * k + half] = term(k + 5, half)
    dx_ref[6] = term(0, 1)
    dx_ref[7] = term(4, 1)
    for copy in stores:
        copy.wait()


def grads(*args):
    vmem = pl.BlockSpec(memory_space=pltpu.VMEM)
    return call(
        grad_kernel,
        (KV, ONE, TWO, TWO, TWO, ONE, jax.ShapeDtypeStruct((8, WIDTH, ROWS), BF)),
        *args,
        out_specs=(pl.BlockSpec(memory_space=pl.ANY),) + (vmem,) * 6,
        scratch=[
            pltpu.SMEM((8, 2 * ROWS), jnp.int32),
            pltpu.VMEM((WIDTH, RUN), BF),
            pltpu.VMEM((RUN, WIDTH), F32),
            pltpu.VMEM((RUN, WIDTH), F32),
            pltpu.VMEM((8, WIDTH, 2 * ROWS), F32),
            pltpu.VMEM((16, 2 * ROWS, WIDTH), BF),
            pltpu.SemaphoreType.DMA((3,)),
        ],
    )


def pair_kernel(d0, d1, d2, d3, d4, got, s0, s1, s2, s3, s4):
    for k, (a, out) in enumerate(((d1, s1), (d2, s2), (d3, s3))):
        out[...] = (a[...].astype(F32) + got[2 * k : 2 * k + 2].astype(F32)).astype(BF)
    s0[...] = (d0[...].astype(F32) + got[6].astype(F32)).astype(BF)
    s4[...] = (d4[...].astype(F32) + got[7].astype(F32)).astype(BF)


def column_kernel(s0, e1, e2, e3, e4, keep, send):
    total = e1[...].astype(F32) + e2[...].astype(F32) + e3[...].astype(F32)
    keep[...] = total[0] + e4[...].astype(F32) + s0[...].astype(F32)
    send[...] = total[1].astype(BF)


def last_kernel(dkv_all, keep, got, dq_ref, dk_ref, dv_ref):
    dkv = dkv_all[0].astype(F32)
    for n in range(1, 16):
        dkv = dkv + dkv_all[n].astype(F32)
    dk_ref[...] = (dkv[:ROWS] * SCALE).astype(BF)
    dv_ref[...] = dkv[ROWS:].astype(BF)
    dq_ref[...] = ((keep[...] + got[...].astype(F32)).T * SCALE).astype(BF)


def on_device(
    queries, key_rows, value_rows, outputs, out_grad, log_sums, doc_lengths, tile_allowed
):
    def swap(x):
        return lax.ppermute(x, "c", [(0, 1), (1, 0)])

    def along_z(x, k, both_ways=True, back=False):
        return lax.ppermute(x, AXES, pairs_along_z(k, both_ways, back))

    own = prep(queries, out_grad, outputs, log_sums.reshape(1, ROWS))
    own_x = swap(own)
    kv_out = spread(key_rows, value_rows)
    kv = lax.all_to_all(kv_out, PLANE, 0, 0, tiled=True)
    both = stack(own, own_x, kv_out)
    mine = [along_z(both, k, back=True) for k in (1, 2, 3)]
    mine.append(along_z(own, 4, both_ways=False, back=True))
    at = plan(doc_lengths, tile_allowed, mine[0])
    theirs = [swap(m) for m in mine[::-1]][::-1]

    q, g, stats = slots(own, own_x, *mine[::-1], *theirs[::-1])
    dkv, d0, d1, d2, d3, d4, dx = grads(kv, q, g, stats, at)
    dkv_all = lax.all_to_all(dkv, PLANE, 0, 0, tiled=True)
    s0, s1, s2, s3, s4 = call(
        pair_kernel, (ONE, TWO, TWO, TWO, ONE), d0, d1, d2, d3, d4, swap(dx), cost=PAIR_COST
    )
    e1, e2, e3 = (along_z(s, k) for k, s in ((1, s1), (2, s2), (3, s3)))
    e4 = along_z(s4, 4, both_ways=False)
    keep, send = call(
        column_kernel,
        (jax.ShapeDtypeStruct((WIDTH, ROWS), F32), ONE),
        s0, e1, e2, e3, e4,
    )
    out = jax.ShapeDtypeStruct((ROWS, WIDTH), BF)
    return call(last_kernel, (out, out, out), dkv_all, keep, swap(send))


def solution(mesh):
    fine = Mesh(mesh.devices.reshape(SIZES), AXES)
    rows, vec = P(AXES, None), P(AXES)
    return jax.shard_map(
        on_device,
        mesh=fine,
        in_specs=(rows, rows, rows, rows, rows, vec, P(), P()),
        out_specs=(rows, rows, rows),
        check_vma=False,
    )
```
